32 devices in a mesh: row: 4 (over x, core), col: 8 (over z, y).
Axes of the slice: x: 2, y: 2, z: 4, core: 2. Of those that a mesh axis runs over, the one named last changes fastest.
Arguments:
- left_image: bfloat16 [64, 1024], P('row', 'col'), may hold values from -32 to 32, as said below
- right_image: bfloat16 [64, 1024], P('row', 'col'), may hold values from -32 to 32, as said below
- kernel_one: float32 [64, 9], replicated, may hold values from -2 to 2
- bias_one: float32 [64], replicated, may hold values from -1.5 to 1.5
- kernel_two: bfloat16 [9, 64, 64], replicated, may hold values from -0.25 to 0.25
- bias_two: float32 [64], replicated, may hold values from -1.5 to 1.5
- kernel_three: bfloat16 [9, 64, 64], replicated, may hold values from -0.25 to 0.25
- bias_three: float32 [64], replicated, may hold values from -1.5 to 1.5
- block_list: int32 [4, 8, 8], P('row', 'col'), may hold values from 0 to 15, as said below
- block_count: int32 [4, 8], P('row', 'col'), may hold values from 1 to 8, as said below
Outputs:
- disparity: float32 [64, 1024], P('row', 'col')
The draws below stay inside these ranges and needn't reach their ends.
Inputs may be any that keep to these rules, and one draw needn't show every extreme that they name: `left_image`: pixel values. `right_image`: pixel values. `block_list`: in each tile the first block_count entries are distinct and ascending; later entries have no meaning. `block_count`: some tile lists 8 blocks.
All inputs are finite; a program needn't handle non-finite values.
Results may differ from the reference program's by a relative error of at most 0.0025.
The reference program's roundings to bfloat16 on the way (of `first`, `second` and `features`) count: a program that leaves them out, or rounds other values in their place, can miss the bound.
Values may be sent and summed in bfloat16 or wider, within the bound.
No kernel may reach another device: no remote copies, remote signals or barrier semaphores. Data moves between devices by JAX's collectives and lax.ppermute only.
A program may use at most 64 MiB of HBM per device.

```python
import jax
import jax.numpy as jnp
from jax import lax

ROWS_DEV = 16
COLS_DEV = 128
CHANNELS = 64
DBLOCK = 64
SPAN = 4
NBLOCKS = 16
KMAX = 8
HEIGHT = 64
WIDTH = 1024
N_ROW = 4
N_COL = 8


def image_pair(key):
    base = jnp.clip(jax.random.normal(jax.random.fold_in(key, 11), (HEIGHT, WIDTH), jnp.float32), -5.0, 5.0)
    offset = jax.random.randint(jax.random.fold_in(key, 12), (), -SPAN * COLS_DEV, SPAN * COLS_DEV)
    noise_left = jnp.clip(jax.random.normal(jax.random.fold_in(key, 13), (HEIGHT, WIDTH), jnp.float32), -5.0, 5.0)
    noise_right = jnp.clip(jax.random.normal(jax.random.fold_in(key, 14), (HEIGHT, WIDTH), jnp.float32), -5.0, 5.0)
    left = base + 0.3 * noise_left
    right = jnp.roll(base, offset, axis=1) + 0.3 * noise_right
    return (left, right)


def draw_left_image(key, part):
    left, right = image_pair(key)
    return left.astype(jnp.bfloat16)


def draw_right_image(key, part):
    left, right = image_pair(key)
    return right.astype(jnp.bfloat16)


def draw_block_list(key, part):
    keys = jax.random.split(jax.random.fold_in(key, 21), N_ROW * N_COL)
    picks = jax.vmap(lambda k: jnp.sort(jax.random.permutation(k, NBLOCKS)[:KMAX]))(keys)
    return picks.reshape(N_ROW, N_COL, KMAX).astype(jnp.int32)


def draw_block_count(key, part):
    counts = jax.random.randint(jax.random.fold_in(key, 31), (N_ROW * N_COL,), 1, KMAX + 1)
    fullest = jax.random.randint(jax.random.fold_in(key, 32), (), 0, N_ROW * N_COL)
    counts = counts.at[fullest].set(KMAX)
    return counts.reshape(N_ROW, N_COL).astype(jnp.int32)


def bell_draw(key, extent, scale, bound, kind=jnp.bfloat16):
    entries = jax.random.normal(key, extent, jnp.float32) * scale
    return jnp.minimum(jnp.maximum(entries, -bound), bound).astype(kind)


def setup_inputs(seed: int = 0) -> dict:
    splits = jax.random.split(jax.random.key(seed), 11)
    return {
        "left_image": draw_left_image(jax.random.fold_in(splits[10], 71), 0),
        "right_image": draw_right_image(jax.random.fold_in(splits[10], 71), 0),
        "kernel_one": bell_draw(splits[2], (CHANNELS, 9), 9 ** -0.5, 2.0, jnp.float32),
        "bias_one": bell_draw(splits[3], (CHANNELS,), 0.3, 1.5, jnp.float32),
        "kernel_two": bell_draw(splits[4], (9, CHANNELS, CHANNELS), (9 * CHANNELS) ** -0.5, 0.25),
        "bias_two": bell_draw(splits[5], (CHANNELS,), 0.3, 1.5, jnp.float32),
        "kernel_three": bell_draw(splits[6], (9, CHANNELS, CHANNELS), (9 * CHANNELS) ** -0.5, 0.25),
        "bias_three": bell_draw(splits[7], (CHANNELS,), 0.3, 1.5, jnp.float32),
        "block_list": draw_block_list(jax.random.fold_in(splits[10], 71), 0),
        "block_count": draw_block_count(jax.random.fold_in(splits[10], 71), 0),
    }


def convolve(field, kernel):
    return lax.conv_general_dilated(field, kernel, (1, 1), "SAME", dimension_numbers=("NCHW", "OIHW", "NCHW"), precision=lax.Precision.HIGHEST)


def features(image, kernel_one, bias_one, kernel_two, bias_two, kernel_three, bias_three):
    width_c = kernel_one.shape[0]
    field = image.astype(jnp.float32)[None, None]
    first_k = kernel_one.reshape(width_c, 1, 3, 3)
    first = jax.nn.relu(convolve(field, first_k) + bias_one[None, :, None, None]).astype(jnp.bfloat16)
    second_k = kernel_two.astype(jnp.float32).reshape(3, 3, width_c, width_c).transpose(2, 3, 0, 1)
    second = jax.nn.relu(convolve(first.astype(jnp.float32), second_k) + bias_two[None, :, None, None]).astype(jnp.bfloat16)
    third_k = kernel_three.astype(jnp.float32).reshape(3, 3, width_c, width_c).transpose(2, 3, 0, 1)
    third = (convolve(second.astype(jnp.float32), third_k) + bias_three[None, :, None, None]).astype(jnp.bfloat16)
    return third[0]


def tile_scores(left_tile, window, block):
    chans, rows, cols = left_tile.shape
    tiles = cols // block
    left_parts = left_tile.astype(jnp.float32).reshape(chans, rows, tiles, block)
    right_parts = jnp.stack([window[:, :, block * t:block * t + 2 * block] for t in range(tiles)], axis=2).astype(jnp.float32)
    product = jnp.einsum("crtp,crtq->rtpq", left_parts, right_parts, precision=lax.Precision.HIGHEST)
    flat = product.reshape(rows, tiles, block * 2 * block)
    flat = jnp.concatenate([flat, jnp.zeros((rows, tiles, block), jnp.float32)], axis=2)
    skewed = flat.reshape(rows, tiles, block, 2 * block + 1)[:, :, :, 1:block + 1]
    return skewed[:, :, :, ::-1]


def reference(left_image, right_image, kernel_one, bias_one, kernel_two, bias_two, kernel_three, bias_three, block_list, block_count):
    left_feat = features(left_image, kernel_one, bias_one, kernel_two, bias_two, kernel_three, bias_three)
    right_feat = features(right_image, kernel_one, bias_one, kernel_two, bias_two, kernel_three, bias_three)
    margin = SPAN * COLS_DEV + DBLOCK
    padded = jnp.concatenate([right_feat[:, :, WIDTH - margin:], right_feat, right_feat[:, :, :margin]], axis=2)
    scale = CHANNELS ** -0.5

    def one_tile(index):
        row_block = index // N_COL
        col_block = index % N_COL
        left_tile = lax.dynamic_slice(left_feat, (jnp.int32(0), (row_block * ROWS_DEV).astype(jnp.int32), (col_block * COLS_DEV).astype(jnp.int32)), (CHANNELS, ROWS_DEV, COLS_DEV))
        offsets = block_list[row_block, col_block]
        count = block_count[row_block, col_block]
        score_list = []
        disp_list = []
        for entry in range(KMAX):
            shift = (DBLOCK * offsets[entry] - SPAN * COLS_DEV).astype(jnp.int32)
            start = (col_block * COLS_DEV - shift - DBLOCK + margin).astype(jnp.int32)
            window = lax.dynamic_slice(padded, (jnp.int32(0), (row_block * ROWS_DEV).astype(jnp.int32), start), (CHANNELS, ROWS_DEV, COLS_DEV + DBLOCK))
            score = tile_scores(left_tile, window, DBLOCK) * scale
            score_list.append(jnp.where(entry < count, score, jnp.float32(-1e30)))
            disp_list.append(shift.astype(jnp.float32) + jnp.arange(DBLOCK, dtype=jnp.float32))
        scores = jnp.stack(score_list)
        disps = jnp.stack(disp_list)[:, None, None, None, :]
        top = jnp.max(scores, axis=(0, 4), keepdims=True)
        weights = jnp.exp(scores - top)
        total = jnp.sum(weights, axis=(0, 4))
        moment = jnp.sum(weights * disps, axis=(0, 4))
        return (moment / total / COLS_DEV).reshape(ROWS_DEV, COLS_DEV)

    result = lax.map(one_tile, jnp.arange(N_ROW * N_COL, dtype=jnp.int32))
    result = result.reshape(N_ROW, N_COL, ROWS_DEV, COLS_DEV).transpose(0, 2, 1, 3)
    return result.reshape(HEIGHT, WIDTH)
```

```python
import functools
import math

import jax
import jax.numpy as jnp
from jax import lax
from jax.experimental import pallas as pl
from jax.experimental.pallas import tpu as pltpu
from jax.sharding import PartitionSpec as P

DBLOCK = 64
SPAN = 4
SEGS = 16
PAD = 8
NT = (((1,), (1,)), ((), ()))
TN = (((0,), (0,)), ((), ()))
F32 = jnp.float32
BF16 = jnp.bfloat16


def iota(shape, dim):
    return lax.broadcasted_iota(jnp.int32, shape, dim)


class Plan:
    def __init__(self, mesh, rows, cols, chans):
        self.n_row, self.n_col = mesh.shape["row"], mesh.shape["col"]
        self.rows, self.cols, self.chans = rows, cols, chans
        self.ring = self.n_col == 2 * SPAN
        self.tiles = self.n_col if self.ring else 16
        self.width = self.n_col * cols
        self.seg = self.tiles * cols // SEGS
        self.quads = self.seg // 2
        self.seg_left = cols // SEGS
        self.quads_left = self.seg_left // 2
        self.left_at = (self.quads + 2) * SEGS
        self.total = self.left_at + (self.quads_left + 2) * SEGS
        self.points = self.quads * SEGS
        self.lanes = 4 * chans


def prep_kernel(plan, k1_ref, k2_ref, k3_ref, place_ref, list_ref, w1_ref, w2_ref, w3_ref, bias_ref, disp_ref):
    ch = plan.chans
    kernel = k1_ref[...]
    high = kernel.astype(BF16)
    rest = kernel - high.astype(F32)
    middle = rest.astype(BF16)
    low = (rest - middle.astype(F32)).astype(BF16)
    taps = kernel.shape[1]
    w1_ref[...] = jnp.zeros(w1_ref.shape, BF16)
    for part, values in enumerate((high, middle, low)):
        for out in range(4):
            oy, ox = divmod(out, 2)
            row, tap = iota((5 * 64, taps), 0), iota((5 * 64, taps), 1)
            step, px, y = row // 64, (row // 16) % 4, row % 16
            pick = (px == tap % 3 + ox) & (y == 2 * step + oy + tap // 3)
            block = lax.dot_general(
                jnp.where(pick, 1.0, 0.0).astype(BF16), values, NT, preferred_element_type=F32
            ).astype(BF16)
            for step in range(5):
                w1_ref[step, part * 64 : part * 64 + 64, out * ch : out * ch + ch] = block[
                    step * 64 : step * 64 + 64
                ]
    for source, target in ((k2_ref, w2_ref), (k3_ref, w3_ref)):
        turned = [source[tap].astype(F32).T for tap in range(9)]
        nothing = jnp.zeros((ch, ch), F32)
        for py in range(4):
            for px in range(4):
                pieces = []
                for out in range(4):
                    ty, tx = py - out // 2, px - out % 2
                    inside = 0 <= ty < 3 and 0 <= tx < 3
                    pieces.append(turned[3 * ty + tx] if inside else nothing)
                quad, sub = (py // 2) * 2 + px // 2, (py % 2) * 2 + px % 2
                target[quad, sub * ch : sub * ch + ch, :] = jnp.concatenate(pieces, axis=1).astype(BF16)
    col = place_ref[1]
    bits = jnp.int32(0)
    for k in range(list_ref.shape[0]):
        bits = bits | jnp.where(k < place_ref[2], jnp.left_shift(jnp.int32(1), list_ref[k]), 0)
    reach = SPAN * plan.cols
    shape = (plan.points, 4 * SEGS * plan.quads_left)
    m, n = iota(shape, 0), iota(shape, 1)
    per = SEGS * plan.quads_left
    q = (m % SEGS) * plan.seg + 2 * (m // SEGS) + n // (2 * per)
    left = n % per
    p = (left % SEGS) * plan.seg_left + 2 * (left // SEGS) + (n // per) % 2
    if plan.ring:
        d = col * plan.cols + p - q
        d = jnp.where(d < -reach, d + plan.width, d)
        d = jnp.where(d >= reach, d - plan.width, d)
        listed = jnp.right_shift(bits, (d + reach) // DBLOCK) & 1
    else:
        d = 5 * plan.cols + p - q
        inside = (d >= -reach) & (d < reach)
        block = jnp.where(inside, (d + reach) // DBLOCK, 31)
        listed = jnp.where(inside, jnp.right_shift(bits, block) & 1, 0)
    bias_ref[...] = jnp.where(listed > 0, 0.0, -1e30).astype(F32)
    disp_ref[...] = d.astype(F32)


def main_kernel(
    plan, place_ref, g_ref, w1_ref, b_ref, w2_ref, w3_ref, bias_ref, disp_ref, out_ref,
    ext_ref, extl_ref, f_ref, x1_ref, x2_ref, x3_ref, lb_ref, s_ref, tot_ref, mom_ref,
):
    rows, cols, ch = plan.rows, plan.cols, plan.chans
    row, col = place_ref[0], place_ref[1]
    first_row, last_row = row == 0, row == plan.n_row - 1

    shape = (3 * rows, 512)
    v, lane = iota(shape, 0), iota(shape, 1)
    y = 10 * (lane // 256) + lane % 16
    keep = (v == rows - 3 + y) & (y < rows + 6) & (lane % 256 < 192)
    keep = keep & ((v >= rows) | jnp.logical_not(first_row))
    keep = keep & ((v < 2 * rows) | jnp.logical_not(last_row))
    spread = jnp.where(keep, 1.0, 0.0).astype(BF16)

    def fetch(image, tile):
        parts = []
        for dr in (-1, 0, 1):
            at = jnp.clip(row + dr, 0, plan.n_row - 1) * plan.n_col + tile
            parts.append(g_ref[at, image])
        return lax.dot_general(
            jnp.concatenate(parts, axis=0), spread, TN, preferred_element_type=F32
        )

    for t in range(plan.tiles):
        tile = t if plan.ring else lax.rem(col + (t - 5 + plan.n_col), plan.n_col)
        value = fetch(1, tile)
        for k in range(4):
            ext_ref[k, PAD + t * cols : PAD + (t + 1) * cols, :] = value[:, 128 * k : 128 * k + 128]
    for k in range(4):
        ext_ref[k, 0:PAD, :] = jnp.zeros((PAD, 128), F32)
        ext_ref[k, PAD + plan.tiles * cols :, :] = jnp.zeros((PAD, 128), F32)
    for t in range(3):
        tile = lax.rem(col + (t - 1 + plan.n_col), plan.n_col)
        value = fetch(0, tile)
        for k in range(4):
            extl_ref[k, t * cols : (t + 1) * cols, :] = value[:, 128 * k : 128 * k + 128]

    seg_id = iota((SEGS, 1), 0)
    if plan.ring:
        begin = seg_id * plan.seg
    else:
        begin = lax.rem((col + plan.n_col - 5) * cols + seg_id * plan.seg, plan.width)
    edges_right = (
        jnp.where(begin == 0, 0.0, 1.0).astype(F32),
        jnp.where(begin + plan.seg == plan.width, 0.0, 1.0).astype(F32),
    )
    edges_left = (
        jnp.where((col == 0) & (seg_id == 0), 0.0, 1.0).astype(F32),
        jnp.where((col == plan.n_col - 1) & (seg_id == SEGS - 1), 0.0, 1.0).astype(F32),
    )
    areas = (
        (ext_ref, PAD, plan.seg, 0, edges_right),
        (extl_ref, cols, plan.seg_left, plan.left_at, edges_left),
    )
    px_lane = (iota((SEGS, 128), 1) // 16) % 4
    for half in range(2):
        for source, pad, seg, at, edges in areas:
            for c in range(seg // 2 + 2):
                groups = []
                for k in range(2):
                    value = None
                    for px in range(4):
                        x = 2 * c + px - 3
                        piece = source[2 * half + k, pl.ds(pad + x, SEGS, stride=seg), :]
                        if x < 0:
                            piece = piece * edges[0]
                        if x >= seg:
                            piece = piece * edges[1]
                        value = piece if value is None else jnp.where(px_lane == px, piece, value)
                    groups.append(value)
                f_ref[half, at + c * SEGS : at + (c + 1) * SEGS, :] = jnp.concatenate(
                    groups, axis=1
                ).astype(BF16)

    def clear_first(value):
        pieces = []
        for _, _, seg, at, edges in areas:
            end = at + (seg // 2 + 2) * SEGS
            pieces.append(value[at : at + SEGS] * edges[0])
            pieces.append(value[at + SEGS : end - SEGS])
            pieces.append(value[end - SEGS : end] * edges[1])
        return jnp.concatenate(pieces, axis=0)

    for half in range(2):
        def layer_one(step, carry):
            value = jnp.dot(f_ref[half], w1_ref[step], preferred_element_type=F32)
            value = jax.nn.relu(value + b_ref[0:1, :])
            x1_ref[5 * half + step] = clear_first(value).astype(BF16)
            return carry

        lax.fori_loop(0, 5, layer_one, 0)

    @pl.when(first_row)
    def _():
        x1_ref[0] = jnp.zeros(x1_ref.shape[1:], BF16)

    @pl.when(last_row)
    def _():
        x1_ref[9] = jnp.zeros(x1_ref.shape[1:], BF16)

    def four(source, weight, r, count):
        value = jnp.dot(source[r, 0:count], weight[0], preferred_element_type=F32)
        value += jnp.dot(source[r, SEGS : count + SEGS], weight[1], preferred_element_type=F32)
        value += jnp.dot(source[r + 1, 0:count], weight[2], preferred_element_type=F32)
        return value + jnp.dot(source[r + 1, SEGS : count + SEGS], weight[3], preferred_element_type=F32)

    count_two = plan.total - SEGS
    odd = (iota((SEGS, plan.lanes), 1) // ch) % 2

    def layer_two(r, carry):
        value = jax.nn.relu(four(x1_ref, w2_ref, r, count_two) + b_ref[1:2, :])
        x2_ref[r] = value.astype(BF16)
        for _, _, seg, at, edges in areas:
            end = at + (seg // 2 + 1) * SEGS
            head = value[at : at + SEGS]
            x2_ref[r, at : at + SEGS] = jnp.where(odd == 0, head * edges[0], head).astype(BF16)
            tail = value[end - SEGS : end]
            x2_ref[r, end - SEGS : end] = jnp.where(odd == 1, tail * edges[1], tail).astype(BF16)
        return carry

    lax.fori_loop(0, 9, layer_two, 0)

    @pl.when(first_row)
    def _():
        x2_ref[0, :, 0 : 2 * ch] = jnp.zeros((count_two, 2 * ch), BF16)

    @pl.when(last_row)
    def _():
        x2_ref[8, :, 2 * ch :] = jnp.zeros((count_two, 2 * ch), BF16)

    count_three = count_two - SEGS
    per = plan.quads_left * SEGS
    group = iota((per, plan.lanes), 1) // ch

    def layer_three(r, carry):
        value = four(x2_ref, w3_ref, r, count_three) + b_ref[2:3, :]
        x3_ref[r] = value[: plan.points].astype(BF16)
        left = value[plan.left_at : plan.left_at + per]
        swapped = jnp.concatenate(
            [left[:, ch : 2 * ch], left[:, :ch], left[:, 3 * ch :], left[:, 2 * ch : 3 * ch]], axis=1
        )
        for dy in range(2):
            for dxr in range(2):
                for dxl in range(2):
                    block = jnp.where(group == 2 * dy + dxr, left if dxl == dxr else swapped, 0.0)
                    at = (4 * dy + 2 * dxr + dxl) * per
                    lb_ref[r, at : at + per] = block.astype(BF16)
        return carry

    lax.fori_loop(0, 8, layer_three, 0)

    scale = math.log2(math.e) / math.sqrt(ch)
    pair = 2 * per

    def score(r, carry):
        s_ref[...] = lax.dot_general(x3_ref[r], lb_ref[r], NT, preferred_element_type=F32)
        for dy in range(2):
            lanes = slice(dy * 2 * pair, (dy + 1) * 2 * pair)

            def find_top(i, top):
                at = pl.ds(pl.multiple_of(i * 32, 32), 32)
                value = s_ref[at, lanes] + bias_ref[at, :]
                s_ref[at, lanes] = value
                return jnp.maximum(top, jnp.max(value.reshape(4, 8, 2 * pair), axis=0))

            top = lax.fori_loop(
                0, plan.points // 32, find_top, jnp.full((8, 2 * pair), -1e30, F32), unroll=4
            )
            top = jnp.max(top, axis=0, keepdims=True)
            top = jnp.maximum(top[:, :pair], top[:, pair:])
            top = jnp.broadcast_to(jnp.concatenate([top, top], axis=1), (8, 2 * pair))

            def add_up(i, state):
                total, moment = state
                at = pl.ds(pl.multiple_of(i * 32, 32), 32)
                value = s_ref[at, lanes].reshape(4, 8, 2 * pair) - top[None]
                weight = jnp.exp2(value * scale)
                total = total + jnp.sum(weight, axis=0)
                moment = moment + jnp.sum(weight * disp_ref[at, :].reshape(4, 8, 2 * pair), axis=0)
                return total, moment

            zero = jnp.zeros((8, 2 * pair), F32)
            total, moment = lax.fori_loop(0, plan.points // 32, add_up, (zero, zero), unroll=4)
            total = jnp.sum(total, axis=0, keepdims=True)
            moment = jnp.sum(moment, axis=0, keepdims=True)
            tot_ref[pl.ds(2 * r + dy, 1), :] = total[:, :pair] + total[:, pair:]
            mom_ref[pl.ds(2 * r + dy, 1), :] = moment[:, :pair] + moment[:, pair:]
        return carry

    lax.fori_loop(0, 8, score, 0)

    n, p = iota((pair, cols), 0), iota((pair, cols), 1)
    left = n % per
    place = (left % SEGS) * plan.seg_left + 2 * (left // SEGS) + n // per
    turn = jnp.where(place == p, 1.0, 0.0).astype(F32)
    value = mom_ref[...] / tot_ref[...] * (1.0 / cols)
    out_ref[...] = jnp.dot(value, turn, precision=lax.Precision.HIGHEST, preferred_element_type=F32)


def solution(mesh):
    def per_device(
        left_image, right_image, kernel_one, bias_one, kernel_two, bias_two,
        kernel_three, bias_three, block_list, block_count,
    ):
        rows, cols = left_image.shape
        ch = kernel_one.shape[0]
        plan = Plan(mesh, rows, cols, ch)
        devices = plan.n_row * plan.n_col
        images = jnp.stack([left_image, right_image])
        gathered = lax.all_to_all(
            jnp.broadcast_to(images, (devices,) + images.shape), ("row", "col"), 0, 0
        )
        place = jnp.stack(
            [lax.axis_index("row"), lax.axis_index("col"), block_count[0, 0]]
        ).astype(jnp.int32)
        vmem = pl.BlockSpec(memory_space=pltpu.VMEM)
        smem = pl.BlockSpec(memory_space=pltpu.SMEM)
        lanes = plan.lanes
        n_left = 4 * SEGS * plan.quads_left
        w1, w2, w3, mask, disp = pl.pallas_call(
            functools.partial(prep_kernel, plan),
            out_shape=(
                jax.ShapeDtypeStruct((5, 256, lanes), BF16),
                jax.ShapeDtypeStruct((4, lanes, lanes), BF16),
                jax.ShapeDtypeStruct((4, lanes, lanes), BF16),
                jax.ShapeDtypeStruct((plan.points, n_left), F32),
                jax.ShapeDtypeStruct((plan.points, n_left), F32),
            ),
            in_specs=[vmem, vmem, vmem, smem, smem],
            out_specs=(vmem,) * 5,
            compiler_params=pltpu.CompilerParams(vmem_limit_bytes=48 * 2**20),
        )(kernel_one, kernel_two, kernel_three, place, block_list.reshape(-1))
        biases = jnp.stack([jnp.tile(b, 4) for b in (bias_one, bias_two, bias_three)])
        return pl.pallas_call(
            functools.partial(main_kernel, plan),
            out_shape=jax.ShapeDtypeStruct((rows, cols), F32),
            in_specs=[smem] + [vmem] * 7,
            out_specs=vmem,
            scratch_shapes=[
                pltpu.VMEM((4, plan.tiles * cols + 2 * PAD, 128), F32),
                pltpu.VMEM((4, 3 * cols, 128), F32),
                pltpu.VMEM((2, plan.total, 256), BF16),
                pltpu.VMEM((10, plan.total, lanes), BF16),
                pltpu.VMEM((9, plan.total - SEGS, lanes), BF16),
                pltpu.VMEM((8, plan.points, lanes), BF16),
                pltpu.VMEM((8, 2 * n_left, lanes), BF16),
                pltpu.VMEM((plan.points, 2 * n_left), F32),
                pltpu.VMEM((rows, cols), F32),
                pltpu.VMEM((rows, cols), F32),
            ],
            compiler_params=pltpu.CompilerParams(vmem_limit_bytes=56 * 2**20),
        )(place, gathered, w1, biases, w2, w3, mask, disp)

    return jax.shard_map(
        per_device,
        mesh=mesh,
        in_specs=(
            P("row", "col"), P("row", "col"), P(), P(), P(), P(), P(), P(),
            P("row", "col", None), P("row", "col"),
        ),
        out_specs=P("row", "col"),
        check_vma=False,
    )
```

```python
import functools
import math

import jax
import jax.numpy as jnp
from jax import lax
from jax.experimental import pallas as pl
from jax.experimental.pallas import tpu as pltpu
from jax.sharding import PartitionSpec as P

DBLOCK = 64
SPAN = 4
SEGS = 16
PAD = 8
NT = (((1,), (1,)), ((), ()))
TN = (((0,), (0,)), ((), ()))
F32 = jnp.float32
BF16 = jnp.bfloat16


def iota(shape, dim):
    return lax.broadcasted_iota(jnp.int32, shape, dim)


class Plan:
    def __init__(self, mesh, rows, cols, chans):
        self.n_row, self.n_col = mesh.shape["row"], mesh.shape["col"]
        self.rows, self.cols, self.chans = rows, cols, chans
        self.ring = self.n_col == 2 * SPAN
        self.tiles = self.n_col if self.ring else 16
        self.width = self.n_col * cols
        self.seg = self.tiles * cols // SEGS
        self.quads = self.seg // 2
        self.seg_left = cols // SEGS
        self.quads_left = self.seg_left // 2
        self.left_at = (self.quads + 2) * SEGS
        self.total = self.left_at + (self.quads_left + 2) * SEGS
        self.points = self.quads * SEGS
        self.lanes = 4 * chans


def prep_kernel(plan, k1_ref, k2_ref, k3_ref, place_ref, list_ref, w1_ref, w2_ref, w3_ref, bias_ref, disp_ref):
    ch = plan.chans
    kernel = k1_ref[...]
    high = kernel.astype(BF16)
    rest = kernel - high.astype(F32)
    middle = rest.astype(BF16)
    low = (rest - middle.astype(F32)).astype(BF16)
    taps = kernel.shape[1]
    w1_ref[...] = jnp.zeros(w1_ref.shape, BF16)
    for part, values in enumerate((high, middle, low)):
        for out in range(4):
            oy, ox = divmod(out, 2)
            row, tap = iota((5 * 64, taps), 0), iota((5 * 64, taps), 1)
            step, px, y = row // 64, (row // 16) % 4, row % 16
            pick = (px == tap % 3 + ox) & (y == 2 * step + oy + tap // 3)
            block = lax.dot_general(
                jnp.where(pick, 1.0, 0.0).astype(BF16), values, NT, preferred_element_type=F32
            ).astype(BF16)
            for step in range(5):
                w1_ref[step, part * 64 : part * 64 + 64, out * ch : out * ch + ch] = block[
                    step * 64 : step * 64 + 64
                ]
    for source, target in ((k2_ref, w2_ref), (k3_ref, w3_ref)):
        turned = [source[tap].astype(F32).T for tap in range(9)]
        nothing = jnp.zeros((ch, ch), F32)
        for py in range(4):
            for px in range(4):
                pieces = []
                for out in range(4):
                    ty, tx = py - out // 2, px - out % 2
                    inside = 0 <= ty < 3 and 0 <= tx < 3
                    pieces.append(turned[3 * ty + tx] if inside else nothing)
                quad, sub = (py // 2) * 2 + px // 2, (py % 2) * 2 + px % 2
                target[quad, sub * ch : sub * ch + ch, :] = jnp.concatenate(pieces, axis=1).astype(BF16)
    col = place_ref[1]
    bits = jnp.int32(0)
    for k in range(list_ref.shape[0]):
        bits = bits | jnp.where(k < place_ref[2], jnp.left_shift(jnp.int32(1), list_ref[k]), 0)
    reach = SPAN * plan.cols
    shape = (plan.points, 4 * SEGS * plan.quads_left)
    m, n = iota(shape, 0), iota(shape, 1)
    per = SEGS * plan.quads_left
    q = (m % SEGS) * plan.seg + 2 * (m // SEGS) + n // (2 * per)
    left = n % per
    p = (left % SEGS) * plan.seg_left + 2 * (left // SEGS) + (n // per) % 2
    if plan.ring:
        d = col * plan.cols + p - q
        d = jnp.where(d < -reach, d + plan.width, d)
        d = jnp.where(d >= reach, d - plan.width, d)
        listed = jnp.right_shift(bits, (d + reach) // DBLOCK) & 1
    else:
        d = 5 * plan.cols + p - q
        inside = (d >= -reach) & (d < reach)
        block = jnp.where(inside, (d + reach) // DBLOCK, 31)
        listed = jnp.where(inside, jnp.right_shift(bits, block) & 1, 0)
    bias_ref[...] = jnp.where(listed > 0, 0.0, -1e30).astype(F32)
    disp_ref[...] = d.astype(F32)


def main_kernel(
    plan, place_ref, g_ref, w1_ref, b_ref, w2_ref, w3_ref, bias_ref, disp_ref, out_ref,
    v_ref, ext_ref, f_ref, x1_ref, x2_ref, x3_ref, lb_ref, s_ref, tot_ref, mom_ref,
):
    rows, cols, ch = plan.rows, plan.cols, plan.chans
    row, col = place_ref[0], place_ref[1]
    first_row, last_row = row == 0, row == plan.n_row - 1

    shape = (3 * rows, 512)
    v, lane = iota(shape, 0), iota(shape, 1)
    y = 10 * (lane // 256) + lane % 16
    keep = (v == rows - 3 + y) & (y < rows + 6) & (lane % 256 < 192)
    keep = keep & ((v >= rows) | jnp.logical_not(first_row))
    keep = keep & ((v < 2 * rows) | jnp.logical_not(last_row))
    spread = jnp.where(keep, 1.0, 0.0).astype(BF16)

    tiles = [(1, t if plan.ring else lax.rem(col + (t - 5 + plan.n_col), plan.n_col)) for t in range(plan.tiles)]
    tiles += [(0, lax.rem(col + (t - 1 + plan.n_col), plan.n_col)) for t in range(3)]
    for at, (image, tile) in enumerate(tiles):
        for dr in range(3):
            source = jnp.clip(row + (dr - 1), 0, plan.n_row - 1) * plan.n_col + tile
            v_ref[dr * rows : (dr + 1) * rows, at * cols : (at + 1) * cols] = g_ref[source, image]
    value = lax.dot_general(v_ref[...], spread, TN, preferred_element_type=F32)
    wide = plan.tiles * cols
    for k in range(4):
        ext_ref[k, 0:PAD, :] = jnp.zeros((PAD, 128), F32)
        ext_ref[k, PAD : PAD + wide, :] = value[:wide, 128 * k : 128 * k + 128]
        ext_ref[k, PAD + wide : 2 * PAD + wide, :] = jnp.zeros((PAD, 128), F32)
        ext_ref[k, 2 * PAD + wide :, :] = value[wide:, 128 * k : 128 * k + 128]

    seg_id = iota((SEGS, 1), 0)
    if plan.ring:
        begin = seg_id * plan.seg
    else:
        begin = lax.rem((col + plan.n_col - 5) * cols + seg_id * plan.seg, plan.width)
    edges_right = (
        jnp.where(begin == 0, 0.0, 1.0).astype(F32),
        jnp.where(begin + plan.seg == plan.width, 0.0, 1.0).astype(F32),
    )
    edges_left = (
        jnp.where((col == 0) & (seg_id == 0), 0.0, 1.0).astype(F32),
        jnp.where((col == plan.n_col - 1) & (seg_id == SEGS - 1), 0.0, 1.0).astype(F32),
    )
    areas = (
        (PAD, plan.seg, 0, edges_right),
        (2 * PAD + wide + cols, plan.seg_left, plan.left_at, edges_left),
    )
    px_lane = (iota((SEGS, 128), 1) // 16) % 4

    def gather(pad, seg, at, edges, c):
        known = isinstance(c, int)
        for half in range(2):
            groups = []
            for k in range(2):
                value = None
                for px in range(4):
                    x = 2 * c + px - 3
                    piece = ext_ref[2 * half + k, pl.ds(pad + x, SEGS, stride=seg), :]
                    if known and x < 0:
                        piece = piece * edges[0]
                    if known and x >= seg:
                        piece = piece * edges[1]
                    value = piece if value is None else jnp.where(px_lane == px, piece, value)
                groups.append(value)
            target = pl.ds(at + c * SEGS if known else pl.multiple_of(at + c * SEGS, SEGS), SEGS)
            f_ref[half, target, :] = jnp.concatenate(groups, axis=1).astype(BF16)

    for pad, seg, at, edges in areas:
        quads = seg // 2
        for c in (0, 1, quads, quads + 1):
            gather(pad, seg, at, edges, c)

        def inner(c, carry, pad=pad, seg=seg, at=at, edges=edges):
            gather(pad, seg, at, edges, c)
            return carry

        lax.fori_loop(2, quads, inner, 0, unroll=6 if quads % 6 == 2 else 2)

    def clear_first(value):
        pieces = []
        for _, seg, at, edges in areas:
            end = at + (seg // 2 + 2) * SEGS
            pieces.append(value[at : at + SEGS] * edges[0])
            pieces.append(value[at + SEGS : end - SEGS])
            pieces.append(value[end - SEGS : end] * edges[1])
        return jnp.concatenate(pieces, axis=0)

    pitch = plan.total
    for half in range(2):
        for step in range(5):
            value = jnp.dot(f_ref[half], w1_ref[step], preferred_element_type=F32)
            value = jax.nn.relu(value + b_ref[0:1, :])
            at = (5 * half + step) * pitch
            x1_ref[at : at + pitch] = clear_first(value).astype(BF16)

    @pl.when(first_row)
    def _():
        x1_ref[0:pitch] = jnp.zeros((pitch, plan.lanes), BF16)

    @pl.when(last_row)
    def _():
        x1_ref[9 * pitch :] = jnp.zeros((pitch, plan.lanes), BF16)

    def four(source, weight, start, count):
        value = None
        for k in range(4):
            at = pl.multiple_of(start + (k // 2) * pitch + (k % 2) * SEGS, SEGS)
            part = jnp.dot(source[pl.ds(at, count)], weight[k], preferred_element_type=F32)
            value = part if value is None else value + part
        return value

    odd = (iota((SEGS, plan.lanes), 1) // ch) % 2

    def layer_two(i, carry):
        start = i * (3 * pitch)
        value = four(x1_ref, w2_ref, start, 3 * pitch - SEGS)
        value = jax.nn.relu(value + b_ref[1:2, :])
        x2_ref[pl.ds(pl.multiple_of(start, SEGS), 3 * pitch - SEGS)] = value.astype(BF16)
        for k in range(3):
            for _, seg, at, edges in areas:
                for low in (True, False):
                    base = k * pitch + at + (0 if low else (seg // 2) * SEGS)
                    piece = value[base : base + SEGS]
                    piece = jnp.where(odd == (0 if low else 1), piece * edges[0 if low else 1], piece)
                    x2_ref[pl.ds(pl.multiple_of(start + base, SEGS), SEGS)] = piece.astype(BF16)
        return carry

    lax.fori_loop(0, 3, layer_two, 0)

    @pl.when(first_row)
    def _():
        x2_ref[0:pitch, 0 : 2 * ch] = jnp.zeros((pitch, 2 * ch), BF16)

    @pl.when(last_row)
    def _():
        x2_ref[8 * pitch :, 2 * ch :] = jnp.zeros((pitch, 2 * ch), BF16)

    per = plan.quads_left * SEGS
    group = iota((per, plan.lanes), 1) // ch

    def layer_three(i, carry):
        value = four(x2_ref, w3_ref, i * (2 * pitch), 2 * pitch - 2 * SEGS) + b_ref[2:3, :]
        for k in range(2):
            x3_ref[2 * i + k] = value[k * pitch : k * pitch + plan.points].astype(BF16)
            left = value[k * pitch + plan.left_at : k * pitch + plan.left_at + per]
            swapped = jnp.concatenate(
                [left[:, ch : 2 * ch], left[:, :ch], left[:, 3 * ch :], left[:, 2 * ch : 3 * ch]], axis=1
            )
            for block in range(8):
                dy, dxr, dxl = block // 4, (block // 2) % 2, block % 2
                piece = jnp.where(group == 2 * dy + dxr, left if dxl == dxr else swapped, 0.0)
                lb_ref[2 * i + k, block * per : (block + 1) * per] = piece.astype(BF16)
        return carry

    lax.fori_loop(0, 4, layer_three, 0)

    scale = math.log2(math.e) / math.sqrt(ch)
    pair = 2 * per
    chunk = 32

    def multiply(r, slot):
        value = lax.dot_general(x3_ref[r], lb_ref[r], NT, preferred_element_type=F32)
        tops = []
        for dy in range(2):
            lanes = slice(dy * 2 * pair, (dy + 1) * 2 * pair)
            top = None
            for at in range(0, plan.points, chunk):
                piece = value[at : at + chunk, lanes] + bias_ref[at : at + chunk, :]
                s_ref[slot, at : at + chunk, lanes] = piece
                best = jnp.max(piece.reshape(chunk // 8, 8, 2 * pair), axis=0)
                top = best if top is None else jnp.maximum(top, best)
            top = jnp.max(top, axis=0, keepdims=True)
            top = jnp.maximum(top[:, :pair], top[:, pair:])
            tops.append(jnp.broadcast_to(jnp.concatenate([top, top], axis=1), (8, 2 * pair)))
        return tuple(tops)

    def weigh(r, slot, tops):
        for dy in range(2):
            lanes = slice(dy * 2 * pair, (dy + 1) * 2 * pair)
            total = moment = jnp.zeros((8, 2 * pair), F32)
            for at in range(0, plan.points, chunk):
                value = s_ref[slot, at : at + chunk, lanes].reshape(chunk // 8, 8, 2 * pair)
                weight = jnp.exp2((value - tops[dy][None]) * scale)
                disp = disp_ref[at : at + chunk, :].reshape(chunk // 8, 8, 2 * pair)
                total = total + jnp.sum(weight, axis=0)
                moment = moment + jnp.sum(weight * disp, axis=0)
            total = jnp.sum(total, axis=0, keepdims=True)
            moment = jnp.sum(moment, axis=0, keepdims=True)
            tot_ref[pl.ds(2 * r + dy, 1), :] = total[:, :pair] + total[:, pair:]
            mom_ref[pl.ds(2 * r + dy, 1), :] = moment[:, :pair] + moment[:, pair:]

    def score(r, tops):
        later = multiply(r, r % 2)
        weigh(r - 1, (r - 1) % 2, tops)
        return later

    weigh(7, 1, lax.fori_loop(1, 8, score, multiply(0, 0)))

    n, p = iota((pair, cols), 0), iota((pair, cols), 1)
    left = n % per
    place = (left % SEGS) * plan.seg_left + 2 * (left // SEGS) + n // per
    turn = jnp.where(place == p, 1.0, 0.0).astype(F32)
    value = mom_ref[...] / tot_ref[...] * (1.0 / cols)
    out_ref[...] = jnp.dot(value, turn, precision=lax.Precision.HIGHEST, preferred_element_type=F32)


def solution(mesh):
    def per_device(
        left_image, right_image, kernel_one, bias_one, kernel_two, bias_two,
        kernel_three, bias_three, block_list, block_count,
    ):
        rows, cols = left_image.shape
        ch = kernel_one.shape[0]
        plan = Plan(mesh, rows, cols, ch)
        devices = plan.n_row * plan.n_col
        images = jnp.stack([left_image, right_image])
        gathered = lax.all_to_all(
            jnp.broadcast_to(images, (devices,) + images.shape), ("row", "col"), 0, 0
        )
        place = jnp.stack(
            [lax.axis_index("row"), lax.axis_index("col"), block_count[0, 0]]
        ).astype(jnp.int32)
        vmem = pl.BlockSpec(memory_space=pltpu.VMEM)
        smem = pl.BlockSpec(memory_space=pltpu.SMEM)
        lanes = plan.lanes
        n_left = 4 * SEGS * plan.quads_left
        w1, w2, w3, mask, disp = pl.pallas_call(
            functools.partial(prep_kernel, plan),
            out_shape=(
                jax.ShapeDtypeStruct((5, 256, lanes), BF16),
                jax.ShapeDtypeStruct((4, lanes, lanes), BF16),
                jax.ShapeDtypeStruct((4, lanes, lanes), BF16),
                jax.ShapeDtypeStruct((plan.points, n_left), F32),
                jax.ShapeDtypeStruct((plan.points, n_left), F32),
            ),
            in_specs=[vmem, vmem, vmem, smem, smem],
            out_specs=(vmem,) * 5,
            compiler_params=pltpu.CompilerParams(vmem_limit_bytes=16 * 2**20),
        )(kernel_one, kernel_two, kernel_three, place, block_list.reshape(-1))
        biases = jnp.stack([jnp.tile(b, 4) for b in (bias_one, bias_two, bias_three)])
        return pl.pallas_call(
            functools.partial(main_kernel, plan),
            out_shape=jax.ShapeDtypeStruct((rows, cols), F32),
            in_specs=[smem] + [vmem] * 7,
            out_specs=vmem,
            scratch_shapes=[
                pltpu.VMEM((3 * rows, (plan.tiles + 3) * cols), BF16),
                pltpu.VMEM((4, (plan.tiles + 3) * cols + 2 * PAD, 128), F32),
                pltpu.VMEM((2, plan.total, 256), BF16),
                pltpu.VMEM((10 * plan.total, lanes), BF16),
                pltpu.VMEM((9 * plan.total, lanes), BF16),
                pltpu.VMEM((8, plan.points, lanes), BF16),
                pltpu.VMEM((8, 2 * n_left, lanes), BF16),
                pltpu.VMEM((2, plan.points, 2 * n_left), F32),
                pltpu.VMEM((rows, cols), F32),
                pltpu.VMEM((rows, cols), F32),
            ],
            compiler_params=pltpu.CompilerParams(vmem_limit_bytes=32 * 2**20),
        )(place, gathered, w1, biases, w2, w3, mask, disp)

    return jax.shard_map(
        per_device,
        mesh=mesh,
        in_specs=(
            P("row", "col"), P("row", "col"), P(), P(), P(), P(), P(), P(),
            P("row", "col", None), P("row", "col"),
        ),
        out_specs=P("row", "col"),
        check_vma=False,
    )
```

```python
import functools
import math

import jax
import jax.numpy as jnp
from jax import lax
from jax.experimental import pallas as pl
from jax.experimental.pallas import tpu as pltpu
from jax.sharding import PartitionSpec as P

DBLOCK = 64
SPAN = 4
SEGS = 16
NT = (((1,), (1,)), ((), ()))
F32 = jnp.float32
BF16 = jnp.bfloat16


def iota(shape, dim):
    return lax.broadcasted_iota(jnp.int32, shape, dim)


class Plan:
    def __init__(self, mesh, rows, cols, chans):
        self.n_row, self.n_col = mesh.shape["row"], mesh.shape["col"]
        self.rows, self.cols, self.chans = rows, cols, chans
        self.ring = self.n_col == 2 * SPAN
        self.tiles = self.n_col if self.ring else 16
        self.width = self.n_col * cols
        self.seg = self.tiles * cols // SEGS
        self.quads = self.seg // 2
        self.seg_left = cols // SEGS
        self.quads_left = self.seg_left // 2
        self.left_at = (self.quads + 2) * SEGS
        self.total = self.left_at + (self.quads_left + 2) * SEGS
        self.points = self.quads * SEGS
        self.lanes = 4 * chans


def prep_kernel(
    plan, k1_ref, b1_ref, k2_ref, b2_ref, k3_ref, b3_ref, place_ref, list_ref,
    w1_ref, w2_ref, w3_ref, b_ref, mask_ref, disp_ref, spread_ref,
):
    ch = plan.chans
    kernel = k1_ref[...]
    high = kernel.astype(BF16)
    rest = kernel - high.astype(F32)
    middle = rest.astype(BF16)
    low = (rest - middle.astype(F32)).astype(BF16)
    taps = kernel.shape[0]
    w1_ref[...] = jnp.zeros(w1_ref.shape, BF16)
    for part, values in enumerate((high, middle, low)):
        for out in range(4):
            oy, ox = divmod(out, 2)
            row, tap = iota((5 * 64, taps), 0), iota((5 * 64, taps), 1)
            step, px, y = row // 64, (row // 16) % 4, row % 16
            pick = (px == tap % 3 + ox) & (y == 2 * step + oy + tap // 3)
            pick = jnp.where(pick, 1.0, 0.0).astype(BF16)
            block = jnp.dot(pick, values, preferred_element_type=F32).astype(BF16)
            for step in range(5):
                w1_ref[step, part * 64 : part * 64 + 64, out * ch : out * ch + ch] = block[
                    step * 64 : step * 64 + 64
                ]
    for layer, bias in enumerate((b1_ref, b2_ref, b3_ref)):
        b_ref[layer : layer + 1, :] = jnp.concatenate([bias[...]] * 4, axis=1)
    for source, target in ((k2_ref, w2_ref), (k3_ref, w3_ref)):
        turned = [source[tap].astype(F32).T for tap in range(9)]
        nothing = jnp.zeros((ch, ch), F32)
        for py in range(4):
            for px in range(4):
                pieces = []
                for out in range(4):
                    ty, tx = py - out // 2, px - out % 2
                    inside = 0 <= ty < 3 and 0 <= tx < 3
                    pieces.append(turned[3 * ty + tx] if inside else nothing)
                quad, sub = (py // 2) * 2 + px // 2, (py % 2) * 2 + px % 2
                at = (4 * quad + sub) * ch
                target[at : at + ch, :] = jnp.concatenate(pieces, axis=1).astype(BF16)
    col = place_ref[1]
    bits = jnp.int32(0)
    for k in range(list_ref.shape[0]):
        bits = bits | jnp.where(k < place_ref[2], jnp.left_shift(jnp.int32(1), list_ref[k]), 0)
    reach = SPAN * plan.cols
    shape = (plan.points, 4 * SEGS * plan.quads_left)
    m, n = iota(shape, 0), iota(shape, 1)
    per = SEGS * plan.quads_left
    q = (m % SEGS) * plan.seg + 2 * (m // SEGS) + n // (2 * per)
    left = n % per
    p = (left % SEGS) * plan.seg_left + 2 * (left // SEGS) + (n // per) % 2
    if plan.ring:
        d = col * plan.cols + p - q
        d = jnp.where(d < -reach, d + plan.width, d)
        d = jnp.where(d >= reach, d - plan.width, d)
        listed = jnp.right_shift(bits, (d + reach) // DBLOCK) & 1
    else:
        d = 5 * plan.cols + p - q
        inside = (d >= -reach) & (d < reach)
        block = jnp.where(inside, (d + reach) // DBLOCK, 31)
        listed = jnp.where(inside, jnp.right_shift(bits, block) & 1, 0)
    mask_ref[...] = jnp.where(listed > 0, 0.0, -1e30).astype(F32)
    disp_ref[...] = d.astype(F32)

    row = place_ref[0]
    k, n = iota((256, 1), 0), iota((1, 512), 1)
    y = 10 * (n // 256) + n % 16
    wanted = jnp.where((y < plan.rows + 6) & (n % 256 < 192), (n // 16) % 4 * 64 + plan.rows - 3 + y, -1)
    v = k % 64
    hidden = ((row == 0) & (v < plan.rows)) | ((row == plan.n_row - 1) & (v >= 2 * plan.rows))
    spread_ref[...] = jnp.where(wanted == jnp.where(hidden, -2, k), 1.0, 0.0).astype(BF16)


def main_kernel(
    plan, place_ref, g_ref, spread_ref, w1_ref, b_ref, w2_ref, w3_ref, mask_at, disp_at, out_ref,
    v_ref, v4_ref, fx_ref, f_ref, x1_ref, x2_ref, x3_ref, lb_ref, s_ref, tot_ref, mom_ref,
    mask_ref, disp_ref, sems,
):
    rows, cols, ch = plan.rows, plan.cols, plan.chans
    row, col = place_ref[0], place_ref[1]
    first_row, last_row = row == 0, row == plan.n_row - 1
    copies = [
        pltpu.make_async_copy(source, target, sems.at[k])
        for k, (source, target) in enumerate(((mask_at, mask_ref), (disp_at, disp_ref)))
    ]
    for copy in copies:
        copy.start()

    tiles = [(1, t if plan.ring else lax.rem(col + (t - 5 + plan.n_col), plan.n_col)) for t in range(plan.tiles)]
    tiles += [(0, lax.rem(col + (t - 1 + plan.n_col), plan.n_col)) for t in range(3)]
    for at, (image, tile) in enumerate(tiles):
        for dr in range(3):
            source = jnp.clip(row + (dr - 1), 0, plan.n_row - 1) * plan.n_col + tile
            v_ref[dr * rows : (dr + 1) * rows, at * cols : (at + 1) * cols] = g_ref[source, image].astype(F32)
    for px in range(4):
        moved = v_ref[...] if px == 1 else pltpu.roll(v_ref[...], (1 - px) % v_ref.shape[1], 1)
        v4_ref[px * 64 : px * 64 + 3 * rows, :] = moved.astype(BF16)
        v4_ref[px * 64 + 3 * rows : px * 64 + 64, :] = jnp.zeros((64 - 3 * rows, v_ref.shape[1]), BF16)
    wide = plan.tiles * cols
    seg_id = iota((SEGS, 1), 0)
    if plan.ring:
        begin = seg_id * plan.seg
    else:
        begin = lax.rem((col + plan.n_col - 5) * cols + seg_id * plan.seg, plan.width)
    edges_right = (
        jnp.where(begin == 0, 0.0, 1.0).astype(F32),
        jnp.where(begin + plan.seg == plan.width, 0.0, 1.0).astype(F32),
    )
    edges_left = (
        jnp.where((col == 0) & (seg_id == 0), 0.0, 1.0).astype(F32),
        jnp.where((col == plan.n_col - 1) & (seg_id == SEGS - 1), 0.0, 1.0).astype(F32),
    )
    areas = (
        (plan.seg, 0, edges_right),
        (plan.seg_left, plan.left_at, edges_left),
    )
    px_lane = iota((SEGS, 256), 1) // 64
    for start, before, size, (seg, at, edges) in ((0, 0, wide, areas[0]), (wide, cols, 3 * cols, areas[1])):
        count = (seg // 2 + 2) * SEGS
        n, k = iota((count, 1), 0), iota((1, size), 1)
        pick = jnp.where(before + (n % SEGS) * seg + 2 * (n // SEGS) - 2 == k, 1.0, 0.0).astype(BF16)
        value = lax.dot_general(pick, v4_ref[:, start : start + size], NT, preferred_element_type=F32)
        fx_ref[at : at + count, :] = value.astype(BF16)
        low = value[SEGS : 2 * SEGS]
        fx_ref[at + SEGS : at + 2 * SEGS, :] = jnp.where(px_lane == 0, low * edges[0], low).astype(BF16)
        high = value[count - 2 * SEGS : count - SEGS]
        fx_ref[at + count - 2 * SEGS : at + count - SEGS, :] = jnp.where(
            px_lane == 3, high * edges[1], high
        ).astype(BF16)
    for half in range(2):
        value = jnp.dot(
            fx_ref[...], spread_ref[:, half * 256 : half * 256 + 256], preferred_element_type=F32
        )
        f_ref[half] = value.astype(BF16)

    def clear_first(value):
        pieces = []
        for seg, at, edges in areas:
            end = at + (seg // 2 + 2) * SEGS
            pieces.append(value[at : at + SEGS] * edges[0])
            pieces.append(value[at + SEGS : end - SEGS])
            pieces.append(value[end - SEGS : end] * edges[1])
        return jnp.concatenate(pieces, axis=0)

    pitch = plan.total

    def layer_one(half, carry):
        for step in range(5):
            value = jnp.dot(f_ref[half], w1_ref[step], preferred_element_type=F32)
            value = clear_first(jax.nn.relu(value + b_ref[0:1, :]))
            x1_ref[pl.ds(pl.multiple_of((5 * half + step) * pitch, SEGS), pitch)] = value.astype(BF16)
        return carry

    lax.fori_loop(0, 2, layer_one, 0)

    @pl.when(first_row)
    def _():
        x1_ref[0:pitch] = jnp.zeros((pitch, plan.lanes), BF16)

    @pl.when(last_row)
    def _():
        x1_ref[9 * pitch :] = jnp.zeros((pitch, plan.lanes), BF16)

    def four(source, weight, start, count):
        value = None
        for k in range(4):
            at = pl.multiple_of(start + (k // 2) * pitch + (k % 2) * SEGS, SEGS)
            part = jnp.dot(source[pl.ds(at, count)], weight[k * 256 : k * 256 + 256], preferred_element_type=F32)
            value = part if value is None else value + part
        return value

    odd = (iota((SEGS, plan.lanes), 1) // ch) % 2

    def layer_two(i, carry):
        start = i * (3 * pitch)
        value = four(x1_ref, w2_ref, start, 3 * pitch - SEGS)
        value = jax.nn.relu(value + b_ref[1:2, :])
        x2_ref[pl.ds(pl.multiple_of(start, SEGS), 3 * pitch - SEGS)] = value.astype(BF16)
        for k in range(3):
            for seg, at, edges in areas:
                for low in (True, False):
                    base = k * pitch + at + (0 if low else (seg // 2) * SEGS)
                    piece = value[base : base + SEGS]
                    piece = jnp.where(odd == (0 if low else 1), piece * edges[0 if low else 1], piece)
                    x2_ref[pl.ds(pl.multiple_of(start + base, SEGS), SEGS)] = piece.astype(BF16)
        return carry

    lax.fori_loop(0, 3, layer_two, 0)

    @pl.when(first_row)
    def _():
        x2_ref[0:pitch, 0 : 2 * ch] = jnp.zeros((pitch, 2 * ch), BF16)

    @pl.when(last_row)
    def _():
        x2_ref[8 * pitch : 9 * pitch, 2 * ch :] = jnp.zeros((pitch, 2 * ch), BF16)

    per = plan.quads_left * SEGS
    group = iota((per, plan.lanes), 1) // ch

    chunk = 256
    chunks = plan.points // chunk

    def patch(r, at, count):
        base = r * pitch + at
        return jnp.concatenate(
            [
                x2_ref[pl.ds(pl.multiple_of(base + (k // 2) * pitch + (k % 2) * SEGS, SEGS), count)]
                for k in range(4)
            ],
            axis=1,
        )

    def layer_three(r, slot, u):
        value = jnp.dot(patch(r, u * chunk, chunk), w3_ref[...], preferred_element_type=F32)
        x3_ref[slot, u * chunk : (u + 1) * chunk] = (value + b_ref[2:3, :]).astype(BF16)

    def layer_three_left(r, slot):
        left = jnp.dot(patch(r, plan.left_at, per), w3_ref[...], preferred_element_type=F32) + b_ref[2:3, :]
        swapped = jnp.concatenate(
            [left[:, ch : 2 * ch], left[:, :ch], left[:, 3 * ch :], left[:, 2 * ch : 3 * ch]], axis=1
        )
        for block in range(8):
            dy, dxr, dxl = block // 4, (block // 2) % 2, block % 2
            piece = jnp.where(group == 2 * dy + dxr, left if dxl == dxr else swapped, 0.0)
            lb_ref[slot, block * per : (block + 1) * per] = piece.astype(BF16)

    scale = math.log2(math.e) / math.sqrt(ch)
    pair = 2 * per
    step = 32

    def multiply(slot, u, top):
        value = lax.dot_general(
            x3_ref[slot, u * chunk : (u + 1) * chunk], lb_ref[slot], NT, preferred_element_type=F32
        )
        for at in range(0, chunk, step):
            row_at = slice(u * chunk + at, u * chunk + at + step)
            mask = mask_ref[row_at, :]
            piece = value[at : at + step] + jnp.concatenate([mask, mask], axis=1)
            s_ref[slot, row_at, :] = piece
            best = jnp.max(piece.reshape(step // 8, 8, 4 * pair), axis=0)
            top = best if top is None else jnp.maximum(top, best)
        return top

    def spread_top(top):
        top = jnp.max(top, axis=0, keepdims=True)
        parts = []
        for dy in range(2):
            low, high = top[:, 2 * dy * pair : (2 * dy + 1) * pair], top[:, (2 * dy + 1) * pair : (2 * dy + 2) * pair]
            parts += [jnp.maximum(low, high)] * 2
        return jnp.broadcast_to(jnp.concatenate(parts, axis=1), (8, 4 * pair))

    def weigh(slot, u, top, state):
        state = list(state)
        for at in range(0, chunk, step):
            row_at = slice(u * chunk + at, u * chunk + at + step)
            disp = disp_ref[row_at, :].reshape(step // 8, 8, 2 * pair)
            for dy in range(2):
                lanes = slice(dy * 2 * pair, (dy + 1) * 2 * pair)
                value = s_ref[slot, row_at, lanes].reshape(step // 8, 8, 2 * pair)
                weight = jnp.exp2((value - top[:, lanes][None]) * scale)
                state[2 * dy] = state[2 * dy] + jnp.sum(weight, axis=0)
                state[2 * dy + 1] = state[2 * dy + 1] + jnp.sum(weight * disp, axis=0)
        return state

    def keep_sums(r, state):
        for dy in range(2):
            for target, value in ((tot_ref, state[2 * dy]), (mom_ref, state[2 * dy + 1])):
                value = jnp.sum(value, axis=0, keepdims=True)
                target[pl.ds(2 * r + 2 + dy, 1), :] = value[:, :pair] + value[:, pair:]

    none = [jnp.zeros((8, 2 * pair), F32)] * 4
    layer_three_left(0, 0)
    for u in range(chunks):
        layer_three(0, 0, u)
    for copy in copies:
        copy.wait()

    def together(j, top):
        for k in range(2):
            state, later = none, None
            layer_three_left(2 * j + k + 1, 1 - k)
            for u in range(chunks):
                layer_three(2 * j + k + 1, 1 - k, u)
                state = weigh(1 - k, u, top, state)
                later = multiply(k, u, later)
            keep_sums(2 * j + k - 1, state)
            top = spread_top(later)
        return top

    top = lax.fori_loop(0, 4, together, jnp.zeros((8, 4 * pair), F32))
    state = none
    for u in range(chunks):
        state = weigh(1, u, top, state)
    keep_sums(7, state)

    n, p = iota((pair, cols), 0), iota((pair, cols), 1)
    left = n % per
    place = (left % SEGS) * plan.seg_left + 2 * (left // SEGS) + n // per
    turn = jnp.where(place == p, 1.0, 0.0).astype(F32)
    value = mom_ref[2 : rows + 2, :] / tot_ref[2 : rows + 2, :] * (1.0 / cols)
    out_ref[...] = jnp.dot(value, turn, precision=lax.Precision.HIGHEST, preferred_element_type=F32)


def solution(mesh):
    def per_device(
        left_image, right_image, kernel_one, bias_one, kernel_two, bias_two,
        kernel_three, bias_three, block_list, block_count,
    ):
        rows, cols = left_image.shape
        ch = kernel_one.shape[0]
        plan = Plan(mesh, rows, cols, ch)
        devices = plan.n_row * plan.n_col
        images = jnp.stack([left_image, right_image])
        gathered = lax.all_to_all(
            jnp.broadcast_to(images, (devices,) + images.shape), ("row", "col"), 0, 0
        )
        place = jnp.stack(
            [lax.axis_index("row"), lax.axis_index("col"), block_count[0, 0]]
        ).astype(jnp.int32)
        vmem = pl.BlockSpec(memory_space=pltpu.VMEM)
        smem = pl.BlockSpec(memory_space=pltpu.SMEM)
        lanes = plan.lanes
        n_left = 4 * SEGS * plan.quads_left
        w1, w2, w3, biases, mask, disp, spread = pl.pallas_call(
            functools.partial(prep_kernel, plan),
            out_shape=(
                jax.ShapeDtypeStruct((5, 256, lanes), BF16),
                jax.ShapeDtypeStruct((4 * lanes, lanes), BF16),
                jax.ShapeDtypeStruct((4 * lanes, lanes), BF16),
                jax.ShapeDtypeStruct((3, lanes), F32),
                jax.ShapeDtypeStruct((plan.points, n_left), F32),
                jax.ShapeDtypeStruct((plan.points, n_left), F32),
                jax.ShapeDtypeStruct((256, 512), BF16),
            ),
            in_specs=[vmem] * 6 + [smem, smem],
            out_specs=(vmem,) * 7,
            compiler_params=pltpu.CompilerParams(vmem_limit_bytes=(12 if plan.ring else 24) * 2**20),
        )(
            kernel_one.T, bias_one[None], kernel_two, bias_two[None], kernel_three, bias_three[None],
            place, block_list.reshape(-1),
        )
        return pl.pallas_call(
            functools.partial(main_kernel, plan),
            out_shape=jax.ShapeDtypeStruct((rows, cols), F32),
            in_specs=[smem] + [vmem] * 6 + [pl.BlockSpec(memory_space=pltpu.HBM)] * 2,
            out_specs=vmem,
            scratch_shapes=[
                pltpu.VMEM((3 * rows, (plan.tiles + 3) * cols), F32),
                pltpu.VMEM((256, (plan.tiles + 3) * cols), BF16),
                pltpu.VMEM((plan.total, 256), BF16),
                pltpu.VMEM((2, plan.total, 256), BF16),
                pltpu.VMEM((10 * plan.total, lanes), BF16),
                pltpu.VMEM((10 * plan.total, lanes), BF16),
                pltpu.VMEM((2, plan.points, lanes), BF16),
                pltpu.VMEM((2, 2 * n_left, lanes), BF16),
                pltpu.VMEM((2, plan.points, 2 * n_left), F32),
                pltpu.VMEM((rows + 4, cols), F32),
                pltpu.VMEM((rows + 4, cols), F32),
                pltpu.VMEM((plan.points, n_left), F32),
                pltpu.VMEM((plan.points, n_left), F32),
                pltpu.SemaphoreType.DMA((2,)),
            ],
            compiler_params=pltpu.CompilerParams(vmem_limit_bytes=(18 if plan.ring else 44) * 2**20),
        )(place, gathered, spread, w1, biases, w2, w3, mask, disp)

    return jax.shard_map(
        per_device,
        mesh=mesh,
        in_specs=(
            P("row", "col"), P("row", "col"), P(), P(), P(), P(), P(), P(),
            P("row", "col", None), P("row", "col"),
        ),
        out_specs=P("row", "col"),
        check_vma=False,
    )
```

```python
import functools
import math

import jax
import jax.numpy as jnp
from jax import lax
from jax.experimental import pallas as pl
from jax.experimental.pallas import tpu as pltpu
from jax.sharding import PartitionSpec as P

DBLOCK = 64
SPAN = 4
SEGS = 16
NT = (((1,), (1,)), ((), ()))
F32 = jnp.float32
BF16 = jnp.bfloat16


def iota(shape, dim):
    return lax.broadcasted_iota(jnp.int32, shape, dim)


class Plan:
    def __init__(self, mesh, rows, cols, chans):
        self.n_row, self.n_col = mesh.shape["row"], mesh.shape["col"]
        self.rows, self.cols, self.chans = rows, cols, chans
        self.ring = self.n_col == 2 * SPAN
        self.tiles = self.n_col if self.ring else 16
        self.width = self.n_col * cols
        self.seg = self.tiles * cols // SEGS
        self.quads = self.seg // 2
        self.seg_left = cols // SEGS
        self.quads_left = self.seg_left // 2
        self.left_at = (self.quads + 2) * SEGS
        self.total = self.left_at + (self.quads_left + 2) * SEGS
        self.points = self.quads * SEGS
        self.lanes = 4 * chans


def pack_kernel(left_ref, right_ref, out_ref):
    rows, cols = left_ref.shape
    left = left_ref[...]
    edges = []
    for first in (0, cols - 3):
        lane, n = iota((cols, cols), 0), iota((cols, cols), 1)
        pick = jnp.where(lane == first + n // rows, 1.0, 0.0).astype(BF16)
        value = jnp.dot(left, pick, preferred_element_type=F32)
        y, n = iota((rows, cols), 0), iota((rows, cols), 1)
        value = jnp.where((y == n % rows) & (n < 3 * rows), value, 0.0)
        edges.append(jnp.sum(value, axis=0, keepdims=True))
    left = left.astype(F32)
    message = jnp.concatenate(
        [right_ref[...].astype(F32), left[:3], left[rows - 3 :]] + edges, axis=0
    ).astype(BF16)
    for k in range(out_ref.shape[0]):
        out_ref[k] = message


def prep_kernel(
    plan, left_ref, k1_ref, b1_ref, k2_ref, b2_ref, k3_ref, b3_ref, place_ref, list_ref,
    w1_ref, w2_ref, w3_ref, b_ref, mask_ref, disp_ref, spread_ref, own_ref,
):
    ch = plan.chans
    own_ref[...] = left_ref[...].astype(F32)
    kernel = k1_ref[...]
    high = kernel.astype(BF16)
    rest = kernel - high.astype(F32)
    middle = rest.astype(BF16)
    low = (rest - middle.astype(F32)).astype(BF16)
    taps = kernel.shape[0]
    w1_ref[...] = jnp.zeros(w1_ref.shape, BF16)
    for part, values in enumerate((high, middle, low)):
        for out in range(4):
            oy, ox = divmod(out, 2)
            row, tap = iota((5 * 64, taps), 0), iota((5 * 64, taps), 1)
            step, px, y = row // 64, (row // 16) % 4, row % 16
            pick = (px == tap % 3 + ox) & (y == 2 * step + oy + tap // 3)
            pick = jnp.where(pick, 1.0, 0.0).astype(BF16)
            block = jnp.dot(pick, values, preferred_element_type=F32).astype(BF16)
            for step in range(5):
                w1_ref[step, part * 64 : part * 64 + 64, out * ch : out * ch + ch] = block[
                    step * 64 : step * 64 + 64
                ]
    for layer, bias in enumerate((b1_ref, b2_ref, b3_ref)):
        b_ref[layer : layer + 1, :] = jnp.concatenate([bias[...]] * 4, axis=1)
    for source, target in ((k2_ref, w2_ref), (k3_ref, w3_ref)):
        turned = [source[tap].astype(F32).T for tap in range(9)]
        nothing = jnp.zeros((ch, ch), F32)
        for py in range(4):
            for px in range(4):
                pieces = []
                for out in range(4):
                    ty, tx = py - out // 2, px - out % 2
                    inside = 0 <= ty < 3 and 0 <= tx < 3
                    pieces.append(turned[3 * ty + tx] if inside else nothing)
                quad, sub = (py // 2) * 2 + px // 2, (py % 2) * 2 + px % 2
                at = (4 * quad + sub) * ch
                target[at : at + ch, :] = jnp.concatenate(pieces, axis=1).astype(BF16)
    col = place_ref[1]
    bits = jnp.int32(0)
    for k in range(list_ref.shape[0]):
        bits = bits | jnp.where(k < place_ref[2], jnp.left_shift(jnp.int32(1), list_ref[k]), 0)
    reach = SPAN * plan.cols
    shape = (plan.points, 4 * SEGS * plan.quads_left)
    m, n = iota(shape, 0), iota(shape, 1)
    per = SEGS * plan.quads_left
    q = (m % SEGS) * plan.seg + 2 * (m // SEGS) + n // (2 * per)
    left = n % per
    p = (left % SEGS) * plan.seg_left + 2 * (left // SEGS) + (n // per) % 2
    if plan.ring:
        d = col * plan.cols + p - q
        d = jnp.where(d < -reach, d + plan.width, d)
        d = jnp.where(d >= reach, d - plan.width, d)
        listed = jnp.right_shift(bits, (d + reach) // DBLOCK) & 1
    else:
        d = 5 * plan.cols + p - q
        inside = (d >= -reach) & (d < reach)
        block = jnp.where(inside, (d + reach) // DBLOCK, 31)
        listed = jnp.where(inside, jnp.right_shift(bits, block) & 1, 0)
    mask_ref[...] = jnp.where(listed > 0, 0.0, -1e30).astype(F32)
    disp_ref[...] = d.astype(F32)

    row = place_ref[0]
    k, n = iota((256, 1), 0), iota((1, 512), 1)
    y = 10 * (n // 256) + n % 16
    wanted = jnp.where((y < plan.rows + 6) & (n % 256 < 192), (n // 16) % 4 * 64 + plan.rows - 3 + y, -1)
    v = k % 64
    hidden = ((row == 0) & (v < plan.rows)) | ((row == plan.n_row - 1) & (v >= 2 * plan.rows))
    spread_ref[...] = jnp.where(wanted == jnp.where(hidden, -2, k), 1.0, 0.0).astype(BF16)


def main_kernel(
    plan, place_ref, g_ref, left_ref, spread_ref, w1_ref, b_ref, w2_ref, w3_ref, mask_ref, disp_ref, out_ref,
    v_ref, v4_ref, fx_ref, f_ref, x1_ref, x2_ref, x3_ref, lb_ref, s_ref, tot_ref, mom_ref,
):
    rows, cols, ch = plan.rows, plan.cols, plan.chans
    row, col = place_ref[0], place_ref[1]
    first_row, last_row = row == 0, row == plan.n_row - 1

    def message(dr, tile):
        return g_ref[jnp.clip(row + dr, 0, plan.n_row - 1) * plan.n_col + tile].astype(F32)

    wide = plan.tiles * cols
    for t in range(plan.tiles):
        tile = t if plan.ring else lax.rem(col + (t - 5 + plan.n_col), plan.n_col)
        for dr in range(3):
            v_ref[dr * rows : (dr + 1) * rows, t * cols : (t + 1) * cols] = message(dr - 1, tile)[:rows]
    blank = jnp.zeros((rows - 3, cols), F32)
    for t in range(3):
        tile = lax.rem(col + (t - 1 + plan.n_col), plan.n_col)
        at = slice(wide + t * cols, wide + (t + 1) * cols)
        v_ref[0:rows, at] = jnp.concatenate([blank, message(-1, tile)[rows + 3 : rows + 6]], axis=0)
        v_ref[2 * rows : 3 * rows, at] = jnp.concatenate([message(1, tile)[rows : rows + 3], blank], axis=0)
        if t == 1:
            v_ref[rows : 2 * rows, at] = left_ref[...]
        else:
            edge = jnp.broadcast_to(message(0, tile)[rows + (7 if t == 0 else 6) :][:1], (rows, cols))
            y, n = iota((rows, cols), 0), iota((rows, cols), 1)
            edge = jnp.where((y == n % rows) & (n < 3 * rows), edge, 0.0).astype(BF16)
            n, lane = iota((cols, cols), 0), iota((cols, cols), 1)
            pick = jnp.where((lane == (cols - 3 if t == 0 else 0) + n // rows) & (n < 3 * rows), 1.0, 0.0)
            v_ref[rows : 2 * rows, at] = jnp.dot(edge, pick.astype(BF16), preferred_element_type=F32)
    for px in range(4):
        moved = v_ref[...] if px == 1 else pltpu.roll(v_ref[...], (1 - px) % v_ref.shape[1], 1)
        v4_ref[px * 64 : px * 64 + 3 * rows, :] = moved.astype(BF16)
        v4_ref[px * 64 + 3 * rows : px * 64 + 64, :] = jnp.zeros((64 - 3 * rows, v_ref.shape[1]), BF16)
    seg_id = iota((SEGS, 1), 0)
    if plan.ring:
        begin = seg_id * plan.seg
    else:
        begin = lax.rem((col + plan.n_col - 5) * cols + seg_id * plan.seg, plan.width)
    edges_right = (
        jnp.where(begin == 0, 0.0, 1.0).astype(F32),
        jnp.where(begin + plan.seg == plan.width, 0.0, 1.0).astype(F32),
    )
    edges_left = (
        jnp.where((col == 0) & (seg_id == 0), 0.0, 1.0).astype(F32),
        jnp.where((col == plan.n_col - 1) & (seg_id == SEGS - 1), 0.0, 1.0).astype(F32),
    )
    areas = (
        (plan.seg, 0, edges_right),
        (plan.seg_left, plan.left_at, edges_left),
    )
    px_lane = iota((SEGS, 256), 1) // 64
    for start, before, size, (seg, at, edges) in ((0, 0, wide, areas[0]), (wide, cols, 3 * cols, areas[1])):
        count = (seg // 2 + 2) * SEGS
        n, k = iota((count, 1), 0), iota((1, size), 1)
        pick = jnp.where(before + (n % SEGS) * seg + 2 * (n // SEGS) - 2 == k, 1.0, 0.0).astype(BF16)
        value = lax.dot_general(pick, v4_ref[:, start : start + size], NT, preferred_element_type=F32)
        fx_ref[at : at + count, :] = value.astype(BF16)
        low = value[SEGS : 2 * SEGS]
        fx_ref[at + SEGS : at + 2 * SEGS, :] = jnp.where(px_lane == 0, low * edges[0], low).astype(BF16)
        high = value[count - 2 * SEGS : count - SEGS]
        fx_ref[at + count - 2 * SEGS : at + count - SEGS, :] = jnp.where(
            px_lane == 3, high * edges[1], high
        ).astype(BF16)
    for half in range(2):
        value = jnp.dot(
            fx_ref[...], spread_ref[:, half * 256 : half * 256 + 256], preferred_element_type=F32
        )
        f_ref[half] = value.astype(BF16)

    def clear_first(value):
        pieces = []
        for seg, at, edges in areas:
            end = at + (seg // 2 + 2) * SEGS
            pieces.append(value[at : at + SEGS] * edges[0])
            pieces.append(value[at + SEGS : end - SEGS])
            pieces.append(value[end - SEGS : end] * edges[1])
        return jnp.concatenate(pieces, axis=0)

    pitch = plan.total

    def layer_one(half, carry):
        for step in range(5):
            value = jnp.dot(f_ref[half], w1_ref[step], preferred_element_type=F32)
            value = clear_first(jax.nn.relu(value + b_ref[0:1, :]))
            x1_ref[pl.ds(pl.multiple_of((5 * half + step) * pitch, SEGS), pitch)] = value.astype(BF16)
        return carry

    lax.fori_loop(0, 2, layer_one, 0)

    @pl.when(first_row)
    def _():
        x1_ref[0:pitch] = jnp.zeros((pitch, plan.lanes), BF16)

    @pl.when(last_row)
    def _():
        x1_ref[9 * pitch :] = jnp.zeros((pitch, plan.lanes), BF16)

    def four(source, weight, start, count):
        value = None
        for k in range(4):
            at = pl.multiple_of(start + (k // 2) * pitch + (k % 2) * SEGS, SEGS)
            part = jnp.dot(source[pl.ds(at, count)], weight[k * 256 : k * 256 + 256], preferred_element_type=F32)
            value = part if value is None else value + part
        return value

    odd = (iota((SEGS, plan.lanes), 1) // ch) % 2

    def layer_two(i, carry):
        start = i * (3 * pitch)
        value = four(x1_ref, w2_ref, start, 3 * pitch - SEGS)
        value = jax.nn.relu(value + b_ref[1:2, :])
        x2_ref[pl.ds(pl.multiple_of(start, SEGS), 3 * pitch - SEGS)] = value.astype(BF16)
        for k in range(3):
            for seg, at, edges in areas:
                for low in (True, False):
                    base = k * pitch + at + (0 if low else (seg // 2) * SEGS)
                    piece = value[base : base + SEGS]
                    piece = jnp.where(odd == (0 if low else 1), piece * edges[0 if low else 1], piece)
                    x2_ref[pl.ds(pl.multiple_of(start + base, SEGS), SEGS)] = piece.astype(BF16)
        return carry

    lax.fori_loop(0, 3, layer_two, 0)

    @pl.when(first_row)
    def _():
        x2_ref[0:pitch, 0 : 2 * ch] = jnp.zeros((pitch, 2 * ch), BF16)

    @pl.when(last_row)
    def _():
        x2_ref[8 * pitch : 9 * pitch, 2 * ch :] = jnp.zeros((pitch, 2 * ch), BF16)

    per = plan.quads_left * SEGS
    group = iota((per, plan.lanes), 1) // ch

    chunk = 256
    chunks = plan.points // chunk

    def patch(r, at, count):
        base = r * pitch + at
        return jnp.concatenate(
            [
                x2_ref[pl.ds(pl.multiple_of(base + (k // 2) * pitch + (k % 2) * SEGS, SEGS), count)]
                for k in range(4)
            ],
            axis=1,
        )

    def layer_three(r, slot, u):
        value = jnp.dot(patch(r, u * chunk, chunk), w3_ref[...], preferred_element_type=F32)
        x3_ref[slot, u * chunk : (u + 1) * chunk] = (value + b_ref[2:3, :]).astype(BF16)

    def layer_three_left(r, slot):
        left = jnp.dot(patch(r, plan.left_at, per), w3_ref[...], preferred_element_type=F32) + b_ref[2:3, :]
        swapped = jnp.concatenate(
            [left[:, ch : 2 * ch], left[:, :ch], left[:, 3 * ch :], left[:, 2 * ch : 3 * ch]], axis=1
        )
        for block in range(8):
            dy, dxr, dxl = block // 4, (block // 2) % 2, block % 2
            piece = jnp.where(group == 2 * dy + dxr, left if dxl == dxr else swapped, 0.0)
            lb_ref[slot, block * per : (block + 1) * per] = piece.astype(BF16)

    scale = math.log2(math.e) / math.sqrt(ch)
    pair = 2 * per
    step = 32

    def multiply(slot, u, top):
        value = lax.dot_general(
            x3_ref[slot, u * chunk : (u + 1) * chunk], lb_ref[slot], NT, preferred_element_type=F32
        )
        for at in range(0, chunk, step):
            row_at = slice(u * chunk + at, u * chunk + at + step)
            mask = mask_ref[row_at, :]
            piece = value[at : at + step] + jnp.concatenate([mask, mask], axis=1)
            s_ref[slot, row_at, :] = piece
            best = jnp.max(piece.reshape(step // 8, 8, 4 * pair), axis=0)
            top = best if top is None else jnp.maximum(top, best)
        return top

    def spread_top(top):
        top = jnp.max(top, axis=0, keepdims=True)
        parts = []
        for dy in range(2):
            low, high = top[:, 2 * dy * pair : (2 * dy + 1) * pair], top[:, (2 * dy + 1) * pair : (2 * dy + 2) * pair]
            parts += [jnp.maximum(low, high)] * 2
        return jnp.broadcast_to(jnp.concatenate(parts, axis=1), (8, 4 * pair))

    def weigh(slot, u, top, state):
        state = list(state)
        for at in range(0, chunk, step):
            row_at = slice(u * chunk + at, u * chunk + at + step)
            disp = disp_ref[row_at, :].reshape(step // 8, 8, 2 * pair)
            for dy in range(2):
                lanes = slice(dy * 2 * pair, (dy + 1) * 2 * pair)
                value = s_ref[slot, row_at, lanes].reshape(step // 8, 8, 2 * pair)
                weight = jnp.exp2((value - top[:, lanes][None]) * scale)
                state[2 * dy] = state[2 * dy] + jnp.sum(weight, axis=0)
                state[2 * dy + 1] = state[2 * dy + 1] + jnp.sum(weight * disp, axis=0)
        return state

    def keep_sums(r, state):
        for dy in range(2):
            for target, value in ((tot_ref, state[2 * dy]), (mom_ref, state[2 * dy + 1])):
                value = jnp.sum(value, axis=0, keepdims=True)
                target[pl.ds(2 * r + 2 + dy, 1), :] = value[:, :pair] + value[:, pair:]

    none = [jnp.zeros((8, 2 * pair), F32)] * 4
    layer_three_left(0, 0)
    for u in range(chunks):
        layer_three(0, 0, u)

    def together(j, top):
        for k in range(2):
            state, later = none, None
            layer_three_left(2 * j + k + 1, 1 - k)
            for u in range(chunks):
                layer_three(2 * j + k + 1, 1 - k, u)
                state = weigh(1 - k, u, top, state)
                later = multiply(k, u, later)
            keep_sums(2 * j + k - 1, state)
            top = spread_top(later)
        return top

    top = lax.fori_loop(0, 4, together, jnp.zeros((8, 4 * pair), F32))
    state = none
    for u in range(chunks):
        state = weigh(1, u, top, state)
    keep_sums(7, state)

    n, p = iota((pair, cols), 0), iota((pair, cols), 1)
    left = n % per
    place = (left % SEGS) * plan.seg_left + 2 * (left // SEGS) + n // per
    turn = jnp.where(place == p, 1.0, 0.0).astype(F32)
    value = mom_ref[2 : rows + 2, :] / tot_ref[2 : rows + 2, :] * (1.0 / cols)
    out_ref[...] = jnp.dot(value, turn, precision=lax.Precision.HIGHEST, preferred_element_type=F32)


def solution(mesh):
    def per_device(
        left_image, right_image, kernel_one, bias_one, kernel_two, bias_two,
        kernel_three, bias_three, block_list, block_count,
    ):
        rows, cols = left_image.shape
        ch = kernel_one.shape[0]
        plan = Plan(mesh, rows, cols, ch)
        devices = plan.n_row * plan.n_col
        message = pl.pallas_call(
            pack_kernel,
            out_shape=jax.ShapeDtypeStruct((devices, rows + 8, cols), BF16),
        )(left_image, right_image)
        gathered = lax.all_to_all(message, ("row", "col"), 0, 0)
        place = jnp.stack(
            [lax.axis_index("row"), lax.axis_index("col"), block_count[0, 0]]
        ).astype(jnp.int32)
        vmem = pl.BlockSpec(memory_space=pltpu.VMEM)
        smem = pl.BlockSpec(memory_space=pltpu.SMEM)
        lanes = plan.lanes
        n_left = 4 * SEGS * plan.quads_left
        w1, w2, w3, biases, mask, disp, spread, own = pl.pallas_call(
            functools.partial(prep_kernel, plan),
            out_shape=(
                jax.ShapeDtypeStruct((5, 256, lanes), BF16),
                jax.ShapeDtypeStruct((4 * lanes, lanes), BF16),
                jax.ShapeDtypeStruct((4 * lanes, lanes), BF16),
                jax.ShapeDtypeStruct((3, lanes), F32),
                jax.ShapeDtypeStruct((plan.points, n_left), F32),
                jax.ShapeDtypeStruct((plan.points, n_left), F32),
                jax.ShapeDtypeStruct((256, 512), BF16),
                jax.ShapeDtypeStruct((rows, cols), F32),
            ),
            in_specs=[vmem] * 7 + [smem, smem],
            out_specs=(vmem,) * 8,
            compiler_params=pltpu.CompilerParams(vmem_limit_bytes=(12 if plan.ring else 24) * 2**20),
        )(
            left_image, kernel_one.T, bias_one[None], kernel_two, bias_two[None], kernel_three, bias_three[None],
            place, block_list.reshape(-1),
        )
        return pl.pallas_call(
            functools.partial(main_kernel, plan),
            out_shape=jax.ShapeDtypeStruct((rows, cols), F32),
            in_specs=[smem] + [vmem] * 9,
            out_specs=vmem,
            scratch_shapes=[
                pltpu.VMEM((3 * rows, (plan.tiles + 3) * cols), F32),
                pltpu.VMEM((256, (plan.tiles + 3) * cols), BF16),
                pltpu.VMEM((plan.total, 256), BF16),
                pltpu.VMEM((2, plan.total, 256), BF16),
                pltpu.VMEM((10 * plan.total, lanes), BF16),
                pltpu.VMEM((10 * plan.total, lanes), BF16),
                pltpu.VMEM((2, plan.points, lanes), BF16),
                pltpu.VMEM((2, 2 * n_left, lanes), BF16),
                pltpu.VMEM((2, plan.points, 2 * n_left), F32),
                pltpu.VMEM((rows + 4, cols), F32),
                pltpu.VMEM((rows + 4, cols), F32),
            ],
            compiler_params=pltpu.CompilerParams(vmem_limit_bytes=(18 if plan.ring else 44) * 2**20),
        )(place, gathered, own, spread, w1, biases, w2, w3, mask, disp)

    return jax.shard_map(
        per_device,
        mesh=mesh,
        in_specs=(
            P("row", "col"), P("row", "col"), P(), P(), P(), P(), P(), P(),
            P("row", "col", None), P("row", "col"),
        ),
        out_specs=P("row", "col"),
        check_vma=False,
    )
```

```python
import functools
import math

import jax
import jax.numpy as jnp
from jax import lax
from jax.experimental import pallas as pl
from jax.experimental.pallas import tpu as pltpu
from jax.sharding import PartitionSpec as P

DBLOCK = 64
SPAN = 4
SEGS = 16
NT = (((1,), (1,)), ((), ()))
F32 = jnp.float32
BF16 = jnp.bfloat16


def iota(shape, dim):
    return lax.broadcasted_iota(jnp.int32, shape, dim)


class Plan:
    def __init__(self, mesh, rows, cols, chans):
        self.n_row, self.n_col = mesh.shape["row"], mesh.shape["col"]
        self.rows, self.cols, self.chans = rows, cols, chans
        self.ring = self.n_col == 2 * SPAN
        self.tiles = self.n_col if self.ring else 16
        self.width = self.n_col * cols
        self.seg = self.tiles * cols // SEGS
        self.quads = self.seg // 2
        self.seg_left = cols // SEGS
        self.quads_left = self.seg_left // 2
        self.left_at = (self.quads + 2) * SEGS
        self.total = self.left_at + (self.quads_left + 2) * SEGS
        self.points = self.quads * SEGS
        self.lanes = 4 * chans


def pack_kernel(left_ref, right_ref, out_ref):
    rows, cols = left_ref.shape
    left = left_ref[...]
    edges = []
    for first in (0, cols - 3):
        lane, n = iota((cols, cols), 0), iota((cols, cols), 1)
        pick = jnp.where(lane == first + n // rows, 1.0, 0.0).astype(BF16)
        value = jnp.dot(left, pick, preferred_element_type=F32)
        y, n = iota((rows, cols), 0), iota((rows, cols), 1)
        value = jnp.where((y == n % rows) & (n < 3 * rows), value, 0.0)
        edges.append(jnp.sum(value, axis=0, keepdims=True))
    left = left.astype(F32)
    message = jnp.concatenate(
        [right_ref[...].astype(F32), left[:3], left[rows - 3 :]] + edges, axis=0
    ).astype(BF16)
    for k in range(out_ref.shape[0]):
        out_ref[k] = message


def prep_kernel(
    plan, left_ref, k1_ref, b1_ref, k2_ref, b2_ref, k3_ref, b3_ref, place_ref, list_ref,
    w1_ref, w2_ref, w3_ref, b_ref, mask_ref, disp_ref, spread_ref, own_ref,
):
    ch = plan.chans
    own_ref[...] = left_ref[...].astype(F32)
    kernel = k1_ref[...]
    high = kernel.astype(BF16)
    rest = kernel - high.astype(F32)
    middle = rest.astype(BF16)
    low = (rest - middle.astype(F32)).astype(BF16)
    taps = kernel.shape[0]
    w1_ref[...] = jnp.zeros(w1_ref.shape, BF16)
    for part, values in enumerate((high, middle, low)):
        for out in range(4):
            oy, ox = divmod(out, 2)
            row, tap = iota((5 * 64, taps), 0), iota((5 * 64, taps), 1)
            step, px, y = row // 64, (row // 16) % 4, row % 16
            pick = (px == tap % 3 + ox) & (y == 2 * step + oy + tap // 3)
            pick = jnp.where(pick, 1.0, 0.0).astype(BF16)
            block = jnp.dot(pick, values, preferred_element_type=F32).astype(BF16)
            for step in range(5):
                w1_ref[step, part * 64 : part * 64 + 64, out * ch : out * ch + ch] = block[
                    step * 64 : step * 64 + 64
                ]
    for layer, bias in enumerate((b1_ref, b2_ref, b3_ref)):
        b_ref[layer : layer + 1, :] = jnp.concatenate([bias[...]] * 4, axis=1)
    for source, target in ((k2_ref, w2_ref), (k3_ref, w3_ref)):
        turned = [source[tap].astype(F32).T for tap in range(9)]
        nothing = jnp.zeros((ch, ch), F32)
        for py in range(4):
            for px in range(4):
                pieces = []
                for out in range(4):
                    ty, tx = py - out // 2, px - out % 2
                    inside = 0 <= ty < 3 and 0 <= tx < 3
                    pieces.append(turned[3 * ty + tx] if inside else nothing)
                quad, sub = (py // 2) * 2 + px // 2, (py % 2) * 2 + px % 2
                at = (4 * quad + sub) * ch
                target[at : at + ch, :] = jnp.concatenate(pieces, axis=1).astype(BF16)
    col = place_ref[1]
    bits = jnp.int32(0)
    for k in range(list_ref.shape[0]):
        bits = bits | jnp.where(k < place_ref[2], jnp.left_shift(jnp.int32(1), list_ref[k]), 0)
    reach = SPAN * plan.cols
    shape = (plan.points, 4 * SEGS * plan.quads_left)
    m, n = iota(shape, 0), iota(shape, 1)
    per = SEGS * plan.quads_left
    q = (m % SEGS) * plan.seg + 2 * (m // SEGS) + n // (2 * per)
    left = n % per
    p = (left % SEGS) * plan.seg_left + 2 * (left // SEGS) + (n // per) % 2
    if plan.ring:
        d = col * plan.cols + p - q
        d = jnp.where(d < -reach, d + plan.width, d)
        d = jnp.where(d >= reach, d - plan.width, d)
        listed = jnp.right_shift(bits, (d + reach) // DBLOCK) & 1
    else:
        d = 5 * plan.cols + p - q
        inside = (d >= -reach) & (d < reach)
        block = jnp.where(inside, (d + reach) // DBLOCK, 31)
        listed = jnp.where(inside, jnp.right_shift(bits, block) & 1, 0)
    mask_ref[...] = jnp.where(listed > 0, 0.0, -1e30).astype(F32)
    disp_ref[...] = d.astype(F32)

    row = place_ref[0]
    k, n = iota((256, 1), 0), iota((1, 512), 1)
    y = 10 * (n // 256) + n % 16
    wanted = jnp.where((y < plan.rows + 6) & (n % 256 < 192), (n // 16) % 4 * 64 + plan.rows - 3 + y, -1)
    v = k % 64
    hidden = ((row == 0) & (v < plan.rows)) | ((row == plan.n_row - 1) & (v >= 2 * plan.rows))
    spread_ref[...] = jnp.where(wanted == jnp.where(hidden, -2, k), 1.0, 0.0).astype(BF16)


def main_kernel(
    plan, place_ref, g_ref, left_ref, spread_ref, w1_ref, b_ref, w2_ref, w3_ref, mask_ref, disp_ref, out_ref,
    v_ref, v4_ref, fx_ref, f_ref, x1_ref, x2_ref, x3_ref, lb_ref, s_ref, tot_ref, mom_ref,
):
    rows, cols, ch = plan.rows, plan.cols, plan.chans
    row, col = place_ref[0], place_ref[1]
    first_row, last_row = row == 0, row == plan.n_row - 1

    def message(dr, tile):
        return g_ref[jnp.clip(row + dr, 0, plan.n_row - 1) * plan.n_col + tile].astype(F32)

    wide = plan.tiles * cols
    for t in range(plan.tiles):
        tile = t if plan.ring else lax.rem(col + (t - 5 + plan.n_col), plan.n_col)
        for dr in range(3):
            v_ref[dr * rows : (dr + 1) * rows, t * cols : (t + 1) * cols] = message(dr - 1, tile)[:rows]
    blank = jnp.zeros((rows - 3, cols), F32)
    for t in range(3):
        tile = lax.rem(col + (t - 1 + plan.n_col), plan.n_col)
        at = slice(wide + t * cols, wide + (t + 1) * cols)
        v_ref[0:rows, at] = jnp.concatenate([blank, message(-1, tile)[rows + 3 : rows + 6]], axis=0)
        v_ref[2 * rows : 3 * rows, at] = jnp.concatenate([message(1, tile)[rows : rows + 3], blank], axis=0)
        if t == 1:
            v_ref[rows : 2 * rows, at] = left_ref[...]
        else:
            edge = jnp.broadcast_to(message(0, tile)[rows + (7 if t == 0 else 6) :][:1], (rows, cols))
            y, n = iota((rows, cols), 0), iota((rows, cols), 1)
            edge = jnp.where((y == n % rows) & (n < 3 * rows), edge, 0.0).astype(BF16)
            n, lane = iota((cols, cols), 0), iota((cols, cols), 1)
            pick = jnp.where((lane == (cols - 3 if t == 0 else 0) + n // rows) & (n < 3 * rows), 1.0, 0.0)
            v_ref[rows : 2 * rows, at] = jnp.dot(edge, pick.astype(BF16), preferred_element_type=F32)
    for px in range(4):
        moved = v_ref[...] if px == 1 else pltpu.roll(v_ref[...], (1 - px) % v_ref.shape[1], 1)
        v4_ref[px * 64 : px * 64 + 3 * rows, :] = moved.astype(BF16)
        v4_ref[px * 64 + 3 * rows : px * 64 + 64, :] = jnp.zeros((64 - 3 * rows, v_ref.shape[1]), BF16)
    seg_id = iota((SEGS, 1), 0)
    if plan.ring:
        begin = seg_id * plan.seg
    else:
        begin = lax.rem((col + plan.n_col - 5) * cols + seg_id * plan.seg, plan.width)
    edges_right = (
        jnp.where(begin == 0, 0.0, 1.0).astype(F32),
        jnp.where(begin + plan.seg == plan.width, 0.0, 1.0).astype(F32),
    )
    edges_left = (
        jnp.where((col == 0) & (seg_id == 0), 0.0, 1.0).astype(F32),
        jnp.where((col == plan.n_col - 1) & (seg_id == SEGS - 1), 0.0, 1.0).astype(F32),
    )
    areas = (
        (plan.seg, 0, edges_right),
        (plan.seg_left, plan.left_at, edges_left),
    )
    px_lane = iota((SEGS, 256), 1) // 64
    for start, before, size, (seg, at, edges) in ((0, 0, wide, areas[0]), (wide, cols, 3 * cols, areas[1])):
        count = (seg // 2 + 2) * SEGS
        n, k = iota((count, 1), 0), iota((1, size), 1)
        pick = jnp.where(before + (n % SEGS) * seg + 2 * (n // SEGS) - 2 == k, 1.0, 0.0).astype(BF16)
        value = lax.dot_general(pick, v4_ref[:, start : start + size], NT, preferred_element_type=F32)
        fx_ref[at : at + count, :] = value.astype(BF16)
        low = value[SEGS : 2 * SEGS]
        fx_ref[at + SEGS : at + 2 * SEGS, :] = jnp.where(px_lane == 0, low * edges[0], low).astype(BF16)
        high = value[count - 2 * SEGS : count - SEGS]
        fx_ref[at + count - 2 * SEGS : at + count - SEGS, :] = jnp.where(
            px_lane == 3, high * edges[1], high
        ).astype(BF16)
    for half in range(2):
        value = jnp.dot(
            fx_ref[...], spread_ref[:, half * 256 : half * 256 + 256], preferred_element_type=F32
        )
        f_ref[half] = value.astype(BF16)

    def clear_first(value):
        pieces = []
        for seg, at, edges in areas:
            end = at + (seg // 2 + 2) * SEGS
            pieces.append(value[at : at + SEGS] * edges[0])
            pieces.append(value[at + SEGS : end - SEGS])
            pieces.append(value[end - SEGS : end] * edges[1])
        return jnp.concatenate(pieces, axis=0)

    pitch = plan.total

    def layer_one(half, carry):
        for step in range(5):
            value = jnp.dot(f_ref[half], w1_ref[step], preferred_element_type=F32)
            value = clear_first(jax.nn.relu(value + b_ref[0:1, :]))
            x1_ref[pl.ds(pl.multiple_of((5 * half + step) * pitch, SEGS), pitch)] = value.astype(BF16)
        return carry

    lax.fori_loop(0, 2, layer_one, 0, unroll=2)

    @pl.when(first_row)
    def _():
        x1_ref[0:pitch] = jnp.zeros((pitch, plan.lanes), BF16)

    @pl.when(last_row)
    def _():
        x1_ref[9 * pitch :] = jnp.zeros((pitch, plan.lanes), BF16)

    def four(source, weight, start, count):
        value = None
        for k in range(4):
            at = pl.multiple_of(start + (k // 2) * pitch + (k % 2) * SEGS, SEGS)
            part = jnp.dot(source[pl.ds(at, count)], weight[k * 256 : k * 256 + 256], preferred_element_type=F32)
            value = part if value is None else value + part
        return value

    odd = (iota((SEGS, plan.lanes), 1) // ch) % 2

    def layer_two(i, carry):
        start = i * (3 * pitch)
        value = four(x1_ref, w2_ref, start, 3 * pitch - SEGS)
        value = jax.nn.relu(value + b_ref[1:2, :])
        x2_ref[pl.ds(pl.multiple_of(start, SEGS), 3 * pitch - SEGS)] = value.astype(BF16)
        for k in range(3):
            for seg, at, edges in areas:
                for low in (True, False):
                    base = k * pitch + at + (0 if low else (seg // 2) * SEGS)
                    piece = value[base : base + SEGS]
                    piece = jnp.where(odd == (0 if low else 1), piece * edges[0 if low else 1], piece)
                    x2_ref[pl.ds(pl.multiple_of(start + base, SEGS), SEGS)] = piece.astype(BF16)
        return carry

    lax.fori_loop(0, 3, layer_two, 0)

    @pl.when(first_row)
    def _():
        x2_ref[0:pitch, 0 : 2 * ch] = jnp.zeros((pitch, 2 * ch), BF16)

    @pl.when(last_row)
    def _():
        x2_ref[8 * pitch : 9 * pitch, 2 * ch :] = jnp.zeros((pitch, 2 * ch), BF16)

    per = plan.quads_left * SEGS
    group = iota((per, plan.lanes), 1) // ch

    chunk = 256
    chunks = plan.points // chunk

    def patch(r, at, count):
        base = r * pitch + at
        return jnp.concatenate(
            [
                x2_ref[pl.ds(pl.multiple_of(base + (k // 2) * pitch + (k % 2) * SEGS, SEGS), count)]
                for k in range(4)
            ],
            axis=1,
        )

    def layer_three(r, slot, u):
        rows_in = patch(r, u * chunk, chunk)
        if u == 0:
            rows_in = jnp.concatenate([rows_in, patch(r, plan.left_at, per)], axis=0)
        value = jnp.dot(rows_in, w3_ref[...], preferred_element_type=F32) + b_ref[2:3, :]
        x3_ref[slot, u * chunk : (u + 1) * chunk] = value[:chunk].astype(BF16)
        if u:
            return
        left = value[chunk:]
        swapped = jnp.concatenate(
            [left[:, ch : 2 * ch], left[:, :ch], left[:, 3 * ch :], left[:, 2 * ch : 3 * ch]], axis=1
        )
        for block in range(8):
            dy, dxr, dxl = block // 4, (block // 2) % 2, block % 2
            piece = jnp.where(group == 2 * dy + dxr, left if dxl == dxr else swapped, 0.0)
            lb_ref[slot, block * per : (block + 1) * per] = piece.astype(BF16)

    scale = math.log2(math.e) / math.sqrt(ch)
    pair = 2 * per
    step = 32

    def multiply(slot, u, top):
        value = lax.dot_general(
            x3_ref[slot, u * chunk : (u + 1) * chunk], lb_ref[slot], NT, preferred_element_type=F32
        )
        for at in range(0, chunk, step):
            row_at = slice(u * chunk + at, u * chunk + at + step)
            mask = mask_ref[row_at, :]
            piece = value[at : at + step] + jnp.concatenate([mask, mask], axis=1)
            s_ref[slot, row_at, :] = piece
            best = jnp.max(piece.reshape(step // 8, 8, 4 * pair), axis=0)
            top = best if top is None else jnp.maximum(top, best)
        return top

    def spread_top(top):
        top = jnp.max(top, axis=0, keepdims=True)
        parts = []
        for dy in range(2):
            low, high = top[:, 2 * dy * pair : (2 * dy + 1) * pair], top[:, (2 * dy + 1) * pair : (2 * dy + 2) * pair]
            parts += [jnp.maximum(low, high)] * 2
        return jnp.broadcast_to(jnp.concatenate(parts, axis=1), (8, 4 * pair))

    def weigh(slot, u, top, state):
        state = list(state)
        for at in range(0, chunk, step):
            row_at = slice(u * chunk + at, u * chunk + at + step)
            disp = disp_ref[row_at, :].reshape(step // 8, 8, 2 * pair)
            for dy in range(2):
                lanes = slice(dy * 2 * pair, (dy + 1) * 2 * pair)
                value = s_ref[slot, row_at, lanes].reshape(step // 8, 8, 2 * pair)
                weight = jnp.exp2((value - top[:, lanes][None]) * scale)
                state[2 * dy] = state[2 * dy] + jnp.sum(weight, axis=0)
                state[2 * dy + 1] = state[2 * dy + 1] + jnp.sum(weight * disp, axis=0)
        return state

    def keep_sums(r, state):
        for dy in range(2):
            for target, value in ((tot_ref, state[2 * dy]), (mom_ref, state[2 * dy + 1])):
                value = jnp.sum(value, axis=0, keepdims=True)
                target[pl.ds(2 * r + 2 + dy, 1), :] = value[:, :pair] + value[:, pair:]

    none = [jnp.zeros((8, 2 * pair), F32)] * 4
    for u in range(chunks):
        layer_three(0, 0, u)

    def together(j, top):
        for k in range(2):
            state, later = none, None
            for u in range(chunks):
                layer_three(2 * j + k + 1, 1 - k, u)
                state = weigh(1 - k, u, top, state)
                later = multiply(k, u, later)
            keep_sums(2 * j + k - 1, state)
            top = spread_top(later)
        return top

    top = lax.fori_loop(0, 4, together, jnp.zeros((8, 4 * pair), F32), unroll=4)
    state = none
    for u in range(chunks):
        state = weigh(1, u, top, state)
    keep_sums(7, state)

    n, p = iota((pair, cols), 0), iota((pair, cols), 1)
    left = n % per
    place = (left % SEGS) * plan.seg_left + 2 * (left // SEGS) + n // per
    turn = jnp.where(place == p, 1.0, 0.0).astype(F32)
    value = mom_ref[2 : rows + 2, :] / tot_ref[2 : rows + 2, :] * (1.0 / cols)
    out_ref[...] = jnp.dot(value, turn, precision=lax.Precision.HIGHEST, preferred_element_type=F32)


def solution(mesh):
    def per_device(
        left_image, right_image, kernel_one, bias_one, kernel_two, bias_two,
        kernel_three, bias_three, block_list, block_count,
    ):
        rows, cols = left_image.shape
        ch = kernel_one.shape[0]
        plan = Plan(mesh, rows, cols, ch)
        devices = plan.n_row * plan.n_col
        message = pl.pallas_call(
            pack_kernel,
            out_shape=jax.ShapeDtypeStruct((devices, rows + 8, cols), BF16),
        )(left_image, right_image)
        gathered = lax.all_to_all(message, ("row", "col"), 0, 0)
        place = jnp.stack(
            [lax.axis_index("row"), lax.axis_index("col"), block_count[0, 0]]
        ).astype(jnp.int32)
        vmem = pl.BlockSpec(memory_space=pltpu.VMEM)
        smem = pl.BlockSpec(memory_space=pltpu.SMEM)
        lanes = plan.lanes
        n_left = 4 * SEGS * plan.quads_left
        w1, w2, w3, biases, mask, disp, spread, own = pl.pallas_call(
            functools.partial(prep_kernel, plan),
            out_shape=(
                jax.ShapeDtypeStruct((5, 256, lanes), BF16),
                jax.ShapeDtypeStruct((4 * lanes, lanes), BF16),
                jax.ShapeDtypeStruct((4 * lanes, lanes), BF16),
                jax.ShapeDtypeStruct((3, lanes), F32),
                jax.ShapeDtypeStruct((plan.points, n_left), F32),
                jax.ShapeDtypeStruct((plan.points, n_left), F32),
                jax.ShapeDtypeStruct((256, 512), BF16),
                jax.ShapeDtypeStruct((rows, cols), F32),
            ),
            in_specs=[vmem] * 7 + [smem, smem],
            out_specs=(vmem,) * 8,
            compiler_params=pltpu.CompilerParams(vmem_limit_bytes=(12 if plan.ring else 24) * 2**20),
        )(
            left_image, kernel_one.T, bias_one[None], kernel_two, bias_two[None], kernel_three, bias_three[None],
            place, block_list.reshape(-1),
        )
        return pl.pallas_call(
            functools.partial(main_kernel, plan),
            out_shape=jax.ShapeDtypeStruct((rows, cols), F32),
            in_specs=[smem] + [vmem] * 9,
            out_specs=vmem,
            scratch_shapes=[
                pltpu.VMEM((3 * rows, (plan.tiles + 3) * cols), F32),
                pltpu.VMEM((256, (plan.tiles + 3) * cols), BF16),
                pltpu.VMEM((plan.total, 256), BF16),
                pltpu.VMEM((2, plan.total, 256), BF16),
                pltpu.VMEM((10 * plan.total, lanes), BF16),
                pltpu.VMEM((10 * plan.total, lanes), BF16),
                pltpu.VMEM((2, plan.points, lanes), BF16),
                pltpu.VMEM((2, 2 * n_left, lanes), BF16),
                pltpu.VMEM((2, plan.points, 2 * n_left), F32),
                pltpu.VMEM((rows + 4, cols), F32),
                pltpu.VMEM((rows + 4, cols), F32),
            ],
            compiler_params=pltpu.CompilerParams(vmem_limit_bytes=(18 if plan.ring else 44) * 2**20),
        )(place, gathered, own, spread, w1, biases, w2, w3, mask, disp)

    return jax.shard_map(
        per_device,
        mesh=mesh,
        in_specs=(
            P("row", "col"), P("row", "col"), P(), P(), P(), P(), P(), P(),
            P("row", "col", None), P("row", "col"),
        ),
        out_specs=P("row", "col"),
        check_vma=False,
    )
```

```python
import functools
import math

import jax
import jax.numpy as jnp
from jax import lax
from jax.experimental import pallas as pl
from jax.experimental.pallas import tpu as pltpu
from jax.sharding import PartitionSpec as P

DBLOCK = 64
SPAN = 4
SEGS = 16
NT = (((1,), (1,)), ((), ()))
F32 = jnp.float32
BF16 = jnp.bfloat16


def iota(shape, dim):
    return lax.broadcasted_iota(jnp.int32, shape, dim)


class Plan:
    def __init__(self, mesh, rows, cols, chans):
        self.n_row, self.n_col = mesh.shape["row"], mesh.shape["col"]
        self.rows, self.cols, self.chans = rows, cols, chans
        self.ring = self.n_col == 2 * SPAN
        self.tiles = self.n_col if self.ring else 16
        self.width = self.n_col * cols
        self.seg = self.tiles * cols // SEGS
        self.quads = self.seg // 2
        self.seg_left = cols // SEGS
        self.quads_left = self.seg_left // 2
        self.left_at = (self.quads + 2) * SEGS
        self.total = self.left_at + (self.quads_left + 2) * SEGS
        self.points = self.quads * SEGS
        self.lanes = 4 * chans


def pack_kernel(left_ref, right_ref, out_ref):
    rows, cols = left_ref.shape
    left = left_ref[...]
    edges = []
    for first in (0, cols - 3):
        lane, n = iota((cols, cols), 0), iota((cols, cols), 1)
        pick = jnp.where(lane == first + n // rows, 1.0, 0.0).astype(BF16)
        value = jnp.dot(left, pick, preferred_element_type=F32)
        y, n = iota((rows, cols), 0), iota((rows, cols), 1)
        value = jnp.where((y == n % rows) & (n < 3 * rows), value, 0.0)
        edges.append(jnp.sum(value, axis=0, keepdims=True))
    left = left.astype(F32)
    message = jnp.concatenate(
        [right_ref[...].astype(F32), left[:3], left[rows - 3 :]] + edges, axis=0
    ).astype(BF16)
    for k in range(out_ref.shape[0]):
        out_ref[k] = message


def prep_kernel(
    plan, left_ref, k1_ref, b1_ref, k2_ref, b2_ref, k3_ref, b3_ref, place_ref, list_ref,
    w1_ref, w2_ref, w3_ref, b_ref, mask_ref, disp_ref, spread_ref, own_ref,
):
    ch = plan.chans
    own_ref[...] = left_ref[...].astype(F32)
    kernel = k1_ref[...]
    high = kernel.astype(BF16)
    rest = kernel - high.astype(F32)
    middle = rest.astype(BF16)
    low = (rest - middle.astype(F32)).astype(BF16)
    taps = kernel.shape[0]
    w1_ref[...] = jnp.zeros(w1_ref.shape, BF16)
    for part, values in enumerate((high, middle, low)):
        for out in range(4):
            oy, ox = divmod(out, 2)
            row, tap = iota((5 * 64, taps), 0), iota((5 * 64, taps), 1)
            step, px, y = row // 64, (row // 16) % 4, row % 16
            pick = (px == tap % 3 + ox) & (y == 2 * step + oy + tap // 3)
            pick = jnp.where(pick, 1.0, 0.0).astype(BF16)
            block = jnp.dot(pick, values, preferred_element_type=F32).astype(BF16)
            for step in range(5):
                w1_ref[step, part * 64 : part * 64 + 64, out * ch : out * ch + ch] = block[
                    step * 64 : step * 64 + 64
                ]
    for layer, bias in enumerate((b1_ref, b2_ref, b3_ref)):
        b_ref[layer : layer + 1, :] = jnp.concatenate([bias[...]] * 4, axis=1)
    for source, target in ((k2_ref, w2_ref), (k3_ref, w3_ref)):
        turned = [source[tap].astype(F32).T for tap in range(9)]
        nothing = jnp.zeros((ch, ch), F32)
        for py in range(4):
            for px in range(4):
                pieces = []
                for out in range(4):
                    ty, tx = py - out // 2, px - out % 2
                    inside = 0 <= ty < 3 and 0 <= tx < 3
                    pieces.append(turned[3 * ty + tx] if inside else nothing)
                quad, sub = (py // 2) * 2 + px // 2, (py % 2) * 2 + px % 2
                at = (4 * quad + sub) * ch
                target[at : at + ch, :] = jnp.concatenate(pieces, axis=1).astype(BF16)
    col = place_ref[1]
    bits = jnp.int32(0)
    for k in range(list_ref.shape[0]):
        bits = bits | jnp.where(k < place_ref[2], jnp.left_shift(jnp.int32(1), list_ref[k]), 0)
    reach = SPAN * plan.cols
    shape = (plan.points, 4 * SEGS * plan.quads_left)
    m, n = iota(shape, 0), iota(shape, 1)
    per = SEGS * plan.quads_left
    q = (m % SEGS) * plan.seg + 2 * (m // SEGS) + n // (2 * per)
    left = n % per
    p = (left % SEGS) * plan.seg_left + 2 * (left // SEGS) + (n // per) % 2
    if plan.ring:
        d = col * plan.cols + p - q
        d = jnp.where(d < -reach, d + plan.width, d)
        d = jnp.where(d >= reach, d - plan.width, d)
        listed = jnp.right_shift(bits, (d + reach) // DBLOCK) & 1
    else:
        d = 5 * plan.cols + p - q
        inside = (d >= -reach) & (d < reach)
        block = jnp.where(inside, (d + reach) // DBLOCK, 31)
        listed = jnp.where(inside, jnp.right_shift(bits, block) & 1, 0)
    mask_ref[...] = jnp.where(listed > 0, 0.0, -1e30).astype(F32)
    disp_ref[...] = d.astype(F32)

    row = place_ref[0]
    k, n = iota((256, 1), 0), iota((1, 512), 1)
    y = 10 * (n // 256) + n % 16
    wanted = jnp.where((y < plan.rows + 6) & (n % 256 < 192), (n // 16) % 4 * 64 + plan.rows - 3 + y, -1)
    v = k % 64
    hidden = ((row == 0) & (v < plan.rows)) | ((row == plan.n_row - 1) & (v >= 2 * plan.rows))
    spread_ref[...] = jnp.where(wanted == jnp.where(hidden, -2, k), 1.0, 0.0).astype(BF16)


def main_kernel(
    plan, place_ref, g_ref, left_ref, spread_ref, w1_ref, b_ref, w2_ref, w3_ref, mask_ref, disp_ref, out_ref,
    v_ref, v4_ref, fx_ref, f_ref, x1_ref, x2_ref, x3_ref, lb_ref, s_ref, tot_ref, mom_ref,
):
    rows, cols, ch = plan.rows, plan.cols, plan.chans
    row, col = place_ref[0], place_ref[1]
    first_row, last_row = row == 0, row == plan.n_row - 1

    def message(dr, tile):
        return g_ref[jnp.clip(row + dr, 0, plan.n_row - 1) * plan.n_col + tile].astype(F32)

    wide = plan.tiles * cols
    for t in range(plan.tiles):
        tile = t if plan.ring else lax.rem(col + (t - 5 + plan.n_col), plan.n_col)
        for dr in range(3):
            v_ref[dr * rows : (dr + 1) * rows, t * cols : (t + 1) * cols] = message(dr - 1, tile)[:rows]
    blank = jnp.zeros((rows - 3, cols), F32)
    for t in range(3):
        tile = lax.rem(col + (t - 1 + plan.n_col), plan.n_col)
        at = slice(wide + t * cols, wide + (t + 1) * cols)
        v_ref[0:rows, at] = jnp.concatenate([blank, message(-1, tile)[rows + 3 : rows + 6]], axis=0)
        v_ref[2 * rows : 3 * rows, at] = jnp.concatenate([message(1, tile)[rows : rows + 3], blank], axis=0)
        if t == 1:
            v_ref[rows : 2 * rows, at] = left_ref[...]
        else:
            edge = jnp.broadcast_to(message(0, tile)[rows + (7 if t == 0 else 6) :][:1], (rows, cols))
            y, n = iota((rows, cols), 0), iota((rows, cols), 1)
            edge = jnp.where((y == n % rows) & (n < 3 * rows), edge, 0.0).astype(BF16)
            n, lane = iota((cols, cols), 0), iota((cols, cols), 1)
            pick = jnp.where((lane == (cols - 3 if t == 0 else 0) + n // rows) & (n < 3 * rows), 1.0, 0.0)
            v_ref[rows : 2 * rows, at] = jnp.dot(edge, pick.astype(BF16), preferred_element_type=F32)
    for px in range(4):
        moved = v_ref[...] if px == 1 else pltpu.roll(v_ref[...], (1 - px) % v_ref.shape[1], 1)
        v4_ref[px * 64 : px * 64 + 3 * rows, :] = moved.astype(BF16)
        v4_ref[px * 64 + 3 * rows : px * 64 + 64, :] = jnp.zeros((64 - 3 * rows, v_ref.shape[1]), BF16)
    seg_id = iota((SEGS, 1), 0)
    if plan.ring:
        begin = seg_id * plan.seg
    else:
        begin = lax.rem((col + plan.n_col - 5) * cols + seg_id * plan.seg, plan.width)
    edges_right = (
        jnp.where(begin == 0, 0.0, 1.0).astype(F32),
        jnp.where(begin + plan.seg == plan.width, 0.0, 1.0).astype(F32),
    )
    edges_left = (
        jnp.where((col == 0) & (seg_id == 0), 0.0, 1.0).astype(F32),
        jnp.where((col == plan.n_col - 1) & (seg_id == SEGS - 1), 0.0, 1.0).astype(F32),
    )
    areas = (
        (plan.seg, 0, edges_right),
        (plan.seg_left, plan.left_at, edges_left),
    )
    px_lane = iota((SEGS, 256), 1) // 64
    for start, before, size, (seg, at, edges) in ((0, 0, wide, areas[0]), (wide, cols, 3 * cols, areas[1])):
        count = (seg // 2 + 2) * SEGS
        n, k = iota((count, 1), 0), iota((1, size), 1)
        pick = jnp.where(before + (n % SEGS) * seg + 2 * (n // SEGS) - 2 == k, 1.0, 0.0).astype(BF16)
        value = lax.dot_general(pick, v4_ref[:, start : start + size], NT, preferred_element_type=F32)
        fx_ref[at : at + count, :] = value.astype(BF16)
        low = value[SEGS : 2 * SEGS]
        fx_ref[at + SEGS : at + 2 * SEGS, :] = jnp.where(px_lane == 0, low * edges[0], low).astype(BF16)
        high = value[count - 2 * SEGS : count - SEGS]
        fx_ref[at + count - 2 * SEGS : at + count - SEGS, :] = jnp.where(
            px_lane == 3, high * edges[1], high
        ).astype(BF16)
    for half in range(2):
        value = jnp.dot(
            fx_ref[...], spread_ref[:, half * 256 : half * 256 + 256], preferred_element_type=F32
        )
        f_ref[half] = value.astype(BF16)

    def clear_first(value):
        pieces = []
        for seg, at, edges in areas:
            end = at + (seg // 2 + 2) * SEGS
            pieces.append(value[at : at + SEGS] * edges[0])
            pieces.append(value[at + SEGS : end - SEGS])
            pieces.append(value[end - SEGS : end] * edges[1])
        return jnp.concatenate(pieces, axis=0)

    pitch = plan.total

    top_row = jnp.where(first_row, 0.0, 1.0).astype(F32)
    end_row = jnp.where(last_row, 0.0, 1.0).astype(F32)
    def layer_one(step):
        value = jnp.dot(f_ref[step // 5], w1_ref[step % 5], preferred_element_type=F32)
        value = clear_first(jax.nn.relu(value + b_ref[0:1, :]))
        if step == 0:
            value = value * top_row
        if step == 9:
            value = value * end_row
        x1_ref[step * pitch : (step + 1) * pitch] = value.astype(BF16)


    odd = (iota((SEGS, plan.lanes), 1) // ch) % 2

    half_at = (plan.quads + 1) // 2 * SEGS + 3 * SEGS
    right_end = (plan.quads + 1) * SEGS
    left_end = plan.left_at + (plan.quads_left + 1) * SEGS

    def patch_two(base, pieces):
        parts = []
        for k in range(4):
            at = base + (k // 2) * pitch + (k % 2) * SEGS
            part = [x1_ref[pl.ds(at + low, high - low)] for low, high in pieces]
            parts.append(part[0] if len(part) == 1 else jnp.concatenate(part, axis=0))
        return jnp.concatenate(parts, axis=1)

    def layer_two(r, parts=(0, 1)):
        base = r * pitch if isinstance(r, int) else pl.multiple_of(r * pitch, SEGS)
        for pieces in [(((0, half_at),), ((half_at, right_end), (plan.left_at, left_end)))[p] for p in parts]:
            value = jnp.dot(patch_two(base, pieces), w2_ref[...], preferred_element_type=F32)
            value = jax.nn.relu(value + b_ref[1:2, :])
            if isinstance(r, int) and r in (0, 8):
                group_row = iota((1, plan.lanes), 1) // (2 * ch)
                keep = jnp.where(group_row == r // 8, top_row if r == 0 else end_row, 1.0)
                value = value * keep
            start = 0
            for low, high in pieces:
                piece = value[start : start + high - low]
                start += high - low
                for (seg, at, edges) in areas:
                    end = at + (seg // 2 + 1) * SEGS
                    if low == at:
                        first = piece[:SEGS]
                        piece = jnp.concatenate([jnp.where(odd == 0, first * edges[0], first), piece[SEGS:]], axis=0)
                    if high == end:
                        last = piece[high - low - SEGS :]
                        piece = jnp.concatenate(
                            [piece[: high - low - SEGS], jnp.where(odd == 1, last * edges[1], last)], axis=0
                        )
                x2_ref[pl.ds(base + low, high - low)] = piece.astype(BF16)

    for step in range(5):
        layer_one(step)
    for r in range(4):
        if r + 5 < 10:
            layer_one(r + 5)
        layer_two(r)
    layer_one(9)

    per = plan.quads_left * SEGS
    group = iota((per, plan.lanes), 1) // ch

    chunk = 256
    chunks = plan.points // chunk

    def patch(r, at, count):
        base = r * pitch + at
        return jnp.concatenate(
            [
                x2_ref[pl.ds(pl.multiple_of(base + (k // 2) * pitch + (k % 2) * SEGS, SEGS), count)]
                for k in range(4)
            ],
            axis=1,
        )

    def layer_three(r, slot, u):
        rows_in = patch(r, u * chunk, chunk)
        if u == 0:
            rows_in = jnp.concatenate([rows_in, patch(r, plan.left_at, per)], axis=0)
        value = jnp.dot(rows_in, w3_ref[...], preferred_element_type=F32) + b_ref[2:3, :]
        x3_ref[slot, u * chunk : (u + 1) * chunk] = value[:chunk].astype(BF16)
        if u:
            return
        left = value[chunk:]
        swapped = jnp.concatenate(
            [left[:, ch : 2 * ch], left[:, :ch], left[:, 3 * ch :], left[:, 2 * ch : 3 * ch]], axis=1
        )
        for block in range(8):
            dy, dxr, dxl = block // 4, (block // 2) % 2, block % 2
            piece = jnp.where(group == 2 * dy + dxr, left if dxl == dxr else swapped, 0.0)
            lb_ref[slot, block * per : (block + 1) * per] = piece.astype(BF16)

    scale = math.log2(math.e) / math.sqrt(ch)
    pair = 2 * per
    step = 32

    def multiply(slot, u, top):
        value = lax.dot_general(
            x3_ref[slot, u * chunk : (u + 1) * chunk], lb_ref[slot], NT, preferred_element_type=F32
        )
        for at in range(0, chunk, step):
            row_at = slice(u * chunk + at, u * chunk + at + step)
            mask = mask_ref[row_at, :]
            piece = value[at : at + step] + jnp.concatenate([mask, mask], axis=1)
            s_ref[slot, row_at, :] = piece
            best = jnp.max(piece.reshape(step // 8, 8, 4 * pair), axis=0)
            top = best if top is None else jnp.maximum(top, best)
        return top

    def spread_top(top):
        top = jnp.max(top, axis=0, keepdims=True)
        parts = []
        for dy in range(2):
            low, high = top[:, 2 * dy * pair : (2 * dy + 1) * pair], top[:, (2 * dy + 1) * pair : (2 * dy + 2) * pair]
            parts += [jnp.maximum(low, high)] * 2
        return jnp.broadcast_to(jnp.concatenate(parts, axis=1), (8, 4 * pair))

    def weigh(slot, u, top, state):
        state = list(state)
        for at in range(0, chunk, step):
            row_at = slice(u * chunk + at, u * chunk + at + step)
            disp = disp_ref[row_at, :].reshape(step // 8, 8, 2 * pair)
            for dy in range(2):
                lanes = slice(dy * 2 * pair, (dy + 1) * 2 * pair)
                value = s_ref[slot, row_at, lanes].reshape(step // 8, 8, 2 * pair)
                weight = jnp.exp2((value - top[:, lanes][None]) * scale)
                state[2 * dy] = state[2 * dy] + jnp.sum(weight, axis=0)
                state[2 * dy + 1] = state[2 * dy + 1] + jnp.sum(weight * disp, axis=0)
        return state

    def keep_sums(r, state):
        for dy in range(2):
            for target, value in ((tot_ref, state[2 * dy]), (mom_ref, state[2 * dy + 1])):
                value = jnp.sum(value, axis=0, keepdims=True)
                target[2 * r + dy : 2 * r + dy + 1, :] = value[:, :pair] + value[:, pair:]

    none = [jnp.zeros((8, 2 * pair), F32)] * 4
    for u in range(chunks):
        layer_three(0, 0, u)

    top = None
    for r in range(9):
        slot, state, later = r % 2, none, None
        for u in range(chunks):
            if r + 4 < 9:
                layer_two(r + 4, range(u * 2 // chunks, (u + 1) * 2 // chunks))
            if r < 7:
                layer_three(r + 1, 1 - slot, u)
            if r > 0:
                state = weigh(1 - slot, u, top, state)
            if r < 8:
                later = multiply(slot, u, later)
        if r > 0:
            keep_sums(r - 1, state)
        top = spread_top(later) if r < 8 else None

    n, p = iota((pair, cols), 0), iota((pair, cols), 1)
    left = n % per
    place = (left % SEGS) * plan.seg_left + 2 * (left // SEGS) + n // per
    turn = jnp.where(place == p, 1.0, 0.0).astype(F32)
    value = mom_ref[...] / tot_ref[...] * (1.0 / cols)
    out_ref[...] = jnp.dot(value, turn, precision=lax.Precision.HIGHEST, preferred_element_type=F32)


def solution(mesh):
    def per_device(
        left_image, right_image, kernel_one, bias_one, kernel_two, bias_two,
        kernel_three, bias_three, block_list, block_count,
    ):
        rows, cols = left_image.shape
        ch = kernel_one.shape[0]
        plan = Plan(mesh, rows, cols, ch)
        devices = plan.n_row * plan.n_col
        message = pl.pallas_call(
            pack_kernel,
            out_shape=jax.ShapeDtypeStruct((devices, rows + 8, cols), BF16),
        )(left_image, right_image)
        gathered = lax.all_to_all(message, ("row", "col"), 0, 0)
        place = jnp.stack(
            [lax.axis_index("row"), lax.axis_index("col"), block_count[0, 0]]
        ).astype(jnp.int32)
        vmem = pl.BlockSpec(memory_space=pltpu.VMEM)
        smem = pl.BlockSpec(memory_space=pltpu.SMEM)
        lanes = plan.lanes
        n_left = 4 * SEGS * plan.quads_left
        w1, w2, w3, biases, mask, disp, spread, own = pl.pallas_call(
            functools.partial(prep_kernel, plan),
            out_shape=(
                jax.ShapeDtypeStruct((5, 256, lanes), BF16),
                jax.ShapeDtypeStruct((4 * lanes, lanes), BF16),
                jax.ShapeDtypeStruct((4 * lanes, lanes), BF16),
                jax.ShapeDtypeStruct((3, lanes), F32),
                jax.ShapeDtypeStruct((plan.points, n_left), F32),
                jax.ShapeDtypeStruct((plan.points, n_left), F32),
                jax.ShapeDtypeStruct((256, 512), BF16),
                jax.ShapeDtypeStruct((rows, cols), F32),
            ),
            in_specs=[vmem] * 7 + [smem, smem],
            out_specs=(vmem,) * 8,
            compiler_params=pltpu.CompilerParams(vmem_limit_bytes=(12 if plan.ring else 24) * 2**20),
        )(
            left_image, kernel_one.T, bias_one[None], kernel_two, bias_two[None], kernel_three, bias_three[None],
            place, block_list.reshape(-1),
        )
        return pl.pallas_call(
            functools.partial(main_kernel, plan),
            out_shape=jax.ShapeDtypeStruct((rows, cols), F32),
            in_specs=[smem] + [vmem] * 9,
            out_specs=vmem,
            scratch_shapes=[
                pltpu.VMEM((3 * rows, (plan.tiles + 3) * cols), F32),
                pltpu.VMEM((256, (plan.tiles + 3) * cols), BF16),
                pltpu.VMEM((plan.total, 256), BF16),
                pltpu.VMEM((2, plan.total, 256), BF16),
                pltpu.VMEM((10 * plan.total, lanes), BF16),
                pltpu.VMEM((10 * plan.total, lanes), BF16),
                pltpu.VMEM((2, plan.points, lanes), BF16),
                pltpu.VMEM((2, 2 * n_left, lanes), BF16),
                pltpu.VMEM((2, plan.points, 2 * n_left), F32),
                pltpu.VMEM((rows, cols), F32),
                pltpu.VMEM((rows, cols), F32),
            ],
            compiler_params=pltpu.CompilerParams(vmem_limit_bytes=(18 if plan.ring else 44) * 2**20),
        )(place, gathered, own, spread, w1, biases, w2, w3, mask, disp)

    return jax.shard_map(
        per_device,
        mesh=mesh,
        in_specs=(
            P("row", "col"), P("row", "col"), P(), P(), P(), P(), P(), P(),
            P("row", "col", None), P("row", "col"),
        ),
        out_specs=P("row", "col"),
        check_vma=False,
    )
```

```python
import functools
import math

import jax
import jax.numpy as jnp
from jax import lax
from jax.experimental import pallas as pl
from jax.experimental.pallas import tpu as pltpu
from jax.sharding import PartitionSpec as P

DBLOCK = 64
SPAN = 4
SEGS = 16
NT = (((1,), (1,)), ((), ()))
F32 = jnp.float32
BF16 = jnp.bfloat16


def iota(shape, dim):
    return lax.broadcasted_iota(jnp.int32, shape, dim)


class Plan:
    def __init__(self, mesh, rows, cols, chans):
        self.n_row, self.n_col = mesh.shape["row"], mesh.shape["col"]
        self.rows, self.cols, self.chans = rows, cols, chans
        self.ring = self.n_col == 2 * SPAN
        self.tiles = self.n_col if self.ring else 16
        self.width = self.n_col * cols
        self.seg = self.tiles * cols // SEGS
        self.quads = self.seg // 2
        self.seg_left = cols // SEGS
        self.quads_left = self.seg_left // 2
        self.left_at = (self.quads + 2) * SEGS
        self.total = self.left_at + (self.quads_left + 2) * SEGS
        self.points = self.quads * SEGS
        self.lanes = 4 * chans


def pack_kernel(left_ref, right_ref, out_ref):
    rows, cols = left_ref.shape
    left = left_ref[...]
    edges = []
    for first in (0, cols - 3):
        lane, n = iota((cols, cols), 0), iota((cols, cols), 1)
        pick = jnp.where(lane == first + n // rows, 1.0, 0.0).astype(BF16)
        value = jnp.dot(left, pick, preferred_element_type=F32)
        y, n = iota((rows, cols), 0), iota((rows, cols), 1)
        value = jnp.where((y == n % rows) & (n < 3 * rows), value, 0.0)
        edges.append(jnp.sum(value, axis=0, keepdims=True))
    left = left.astype(F32)
    message = jnp.concatenate(
        [right_ref[...].astype(F32), left[:3], left[rows - 3 :]] + edges, axis=0
    ).astype(BF16)
    for k in range(out_ref.shape[0]):
        out_ref[k] = message


def prep_kernel(
    plan, left_ref, k1_ref, b1_ref, k2_ref, b2_ref, k3_ref, b3_ref, list_ref, count_ref,
    w1_ref, w2_ref, w3_ref, b_ref, mask_ref, disp_ref, spread_ref, own_ref,
):
    ch = plan.chans
    own_ref[...] = left_ref[...].astype(F32)
    kernel = k1_ref[...]
    high = kernel.astype(BF16)
    rest = kernel - high.astype(F32)
    middle = rest.astype(BF16)
    low = (rest - middle.astype(F32)).astype(BF16)
    taps = kernel.shape[0]
    w1_ref[...] = jnp.zeros(w1_ref.shape, BF16)
    for part, values in enumerate((high, middle, low)):
        for out in range(4):
            oy, ox = divmod(out, 2)
            row, tap = iota((5 * 64, taps), 0), iota((5 * 64, taps), 1)
            step, px, y = row // 64, (row // 16) % 4, row % 16
            pick = (px == tap % 3 + ox) & (y == 2 * step + oy + tap // 3)
            pick = jnp.where(pick, 1.0, 0.0).astype(BF16)
            block = jnp.dot(pick, values, preferred_element_type=F32).astype(BF16)
            for step in range(5):
                w1_ref[step, part * 64 : part * 64 + 64, out * ch : out * ch + ch] = block[
                    step * 64 : step * 64 + 64
                ]
    for layer, bias in enumerate((b1_ref, b2_ref, b3_ref)):
        b_ref[layer : layer + 1, :] = jnp.concatenate([bias[...]] * 4, axis=1)
    for source, target in ((k2_ref, w2_ref), (k3_ref, w3_ref)):
        turned = [source[tap].astype(F32).T for tap in range(9)]
        nothing = jnp.zeros((ch, ch), F32)
        for py in range(4):
            for px in range(4):
                pieces = []
                for out in range(4):
                    ty, tx = py - out // 2, px - out % 2
                    inside = 0 <= ty < 3 and 0 <= tx < 3
                    pieces.append(turned[3 * ty + tx] if inside else nothing)
                quad, sub = (py // 2) * 2 + px // 2, (py % 2) * 2 + px % 2
                at = (4 * quad + sub) * ch
                target[at : at + ch, :] = jnp.concatenate(pieces, axis=1).astype(BF16)
    col = lax.axis_index("col")
    bits = jnp.int32(0)
    for k in range(list_ref.shape[0]):
        bits = bits | jnp.where(k < count_ref[0], jnp.left_shift(jnp.int32(1), list_ref[k]), 0)
    reach = SPAN * plan.cols
    shape = (plan.points, 4 * SEGS * plan.quads_left)
    m, n = iota(shape, 0), iota(shape, 1)
    per = SEGS * plan.quads_left
    q = (m % SEGS) * plan.seg + 2 * (m // SEGS) + n // (2 * per)
    left = n % per
    p = (left % SEGS) * plan.seg_left + 2 * (left // SEGS) + (n // per) % 2
    if plan.ring:
        d = col * plan.cols + p - q
        d = jnp.where(d < -reach, d + plan.width, d)
        d = jnp.where(d >= reach, d - plan.width, d)
        listed = jnp.right_shift(bits, (d + reach) // DBLOCK) & 1
    else:
        d = 5 * plan.cols + p - q
        inside = (d >= -reach) & (d < reach)
        block = jnp.where(inside, (d + reach) // DBLOCK, 31)
        listed = jnp.where(inside, jnp.right_shift(bits, block) & 1, 0)
    mask_ref[...] = jnp.where(listed > 0, 0.0, -1e30).astype(F32)
    disp_ref[...] = d.astype(F32)

    row = lax.axis_index("row")
    k, n = iota((256, 1), 0), iota((1, 512), 1)
    y = 10 * (n // 256) + n % 16
    wanted = jnp.where((y < plan.rows + 6) & (n % 256 < 192), (n // 16) % 4 * 64 + plan.rows - 3 + y, -1)
    v = k % 64
    hidden = ((row == 0) & (v < plan.rows)) | ((row == plan.n_row - 1) & (v >= 2 * plan.rows))
    spread_ref[...] = jnp.where(wanted == jnp.where(hidden, -2, k), 1.0, 0.0).astype(BF16)


def main_kernel(
    plan, g_ref, left_ref, spread_ref, w1_ref, b_ref, w2_ref, w3_ref, mask_ref, disp_ref, out_ref,
    v_ref, v4_ref, fx_ref, f_ref, x1_ref, x2_ref, x3_ref, lb_ref, s_ref, tot_ref, mom_ref,
):
    rows, cols, ch = plan.rows, plan.cols, plan.chans
    row, col = lax.axis_index("row"), lax.axis_index("col")
    first_row, last_row = row == 0, row == plan.n_row - 1

    def message(dr, tile):
        return g_ref[jnp.clip(row + dr, 0, plan.n_row - 1) * plan.n_col + tile].astype(F32)

    wide = plan.tiles * cols
    for t in range(plan.tiles):
        tile = t if plan.ring else lax.rem(col + (t - 5 + plan.n_col), plan.n_col)
        for dr in range(3):
            v_ref[dr * rows : (dr + 1) * rows, t * cols : (t + 1) * cols] = message(dr - 1, tile)[:rows]
    seg_id = iota((SEGS, 1), 0)
    if plan.ring:
        begin = seg_id * plan.seg
    else:
        begin = lax.rem((col + plan.n_col - 5) * cols + seg_id * plan.seg, plan.width)
    edges_right = (
        jnp.where(begin == 0, 0.0, 1.0).astype(F32),
        jnp.where(begin + plan.seg == plan.width, 0.0, 1.0).astype(F32),
    )
    edges_left = (
        jnp.where((col == 0) & (seg_id == 0), 0.0, 1.0).astype(F32),
        jnp.where((col == plan.n_col - 1) & (seg_id == SEGS - 1), 0.0, 1.0).astype(F32),
    )
    areas = (
        (plan.seg, 0, edges_right),
        (plan.seg_left, plan.left_at, edges_left),
    )
    px_lane = iota((SEGS, 256), 1) // 64

    def patches(start, before, size, area):
        seg, at, edges = area
        for px in range(4):
            moved = v_ref[:, start : start + size]
            moved = moved if px == 1 else pltpu.roll(moved, (1 - px) % size, 1)
            v4_ref[px * 64 : px * 64 + 3 * rows, start : start + size] = moved.astype(BF16)
            v4_ref[px * 64 + 3 * rows : px * 64 + 64, start : start + size] = jnp.zeros((64 - 3 * rows, size), BF16)
        count = (seg // 2 + 2) * SEGS
        n, k = iota((count, 1), 0), iota((1, size), 1)
        pick = jnp.where(before + (n % SEGS) * seg + 2 * (n // SEGS) - 2 == k, 1.0, 0.0).astype(BF16)
        value = lax.dot_general(pick, v4_ref[:, start : start + size], NT, preferred_element_type=F32)
        fx_ref[at : at + count, :] = value.astype(BF16)
        low = value[SEGS : 2 * SEGS]
        fx_ref[at + SEGS : at + 2 * SEGS, :] = jnp.where(px_lane == 0, low * edges[0], low).astype(BF16)
        high = value[count - 2 * SEGS : count - SEGS]
        fx_ref[at + count - 2 * SEGS : at + count - SEGS, :] = jnp.where(
            px_lane == 3, high * edges[1], high
        ).astype(BF16)

    patches(0, 0, wide, areas[0])
    blank = jnp.zeros((rows - 3, cols), F32)
    for t in range(3):
        tile = lax.rem(col + (t - 1 + plan.n_col), plan.n_col)
        at = slice(wide + t * cols, wide + (t + 1) * cols)
        v_ref[0:rows, at] = jnp.concatenate([blank, message(-1, tile)[rows + 3 : rows + 6]], axis=0)
        v_ref[2 * rows : 3 * rows, at] = jnp.concatenate([message(1, tile)[rows : rows + 3], blank], axis=0)
        if t == 1:
            v_ref[rows : 2 * rows, at] = left_ref[...]
        else:
            edge = jnp.broadcast_to(message(0, tile)[rows + (7 if t == 0 else 6) :][:1], (rows, cols))
            y, n = iota((rows, cols), 0), iota((rows, cols), 1)
            edge = jnp.where((y == n % rows) & (n < 3 * rows), edge, 0.0).astype(BF16)
            n, lane = iota((cols, cols), 0), iota((cols, cols), 1)
            pick = jnp.where((lane == (cols - 3 if t == 0 else 0) + n // rows) & (n < 3 * rows), 1.0, 0.0)
            v_ref[rows : 2 * rows, at] = jnp.dot(edge, pick.astype(BF16), preferred_element_type=F32)
    patches(wide, cols, 3 * cols, areas[1])
    for half in range(2):
        value = jnp.dot(
            fx_ref[...], spread_ref[:, half * 256 : half * 256 + 256], preferred_element_type=F32
        )
        f_ref[half] = value.astype(BF16)

    def clear_first(value):
        pieces = []
        for seg, at, edges in areas:
            end = at + (seg // 2 + 2) * SEGS
            pieces.append(value[at : at + SEGS] * edges[0])
            pieces.append(value[at + SEGS : end - SEGS])
            pieces.append(value[end - SEGS : end] * edges[1])
        return jnp.concatenate(pieces, axis=0)

    pitch = plan.total

    top_row = jnp.where(first_row, 0.0, 1.0).astype(F32)
    end_row = jnp.where(last_row, 0.0, 1.0).astype(F32)
    def layer_one(step):
        value = jnp.dot(f_ref[step // 5], w1_ref[step % 5], preferred_element_type=F32)
        value = clear_first(jax.nn.relu(value + b_ref[0:1, :]))
        if step == 0:
            value = value * top_row
        if step == 9:
            value = value * end_row
        x1_ref[step * pitch : (step + 1) * pitch] = value.astype(BF16)


    odd = (iota((SEGS, plan.lanes), 1) // ch) % 2

    half_at = (plan.quads + 1) // 2 * SEGS + 3 * SEGS
    right_end = (plan.quads + 1) * SEGS
    left_end = plan.left_at + (plan.quads_left + 1) * SEGS

    def patch_two(base, pieces):
        parts = []
        for k in range(4):
            at = base + (k // 2) * pitch + (k % 2) * SEGS
            part = [x1_ref[pl.ds(at + low, high - low)] for low, high in pieces]
            parts.append(part[0] if len(part) == 1 else jnp.concatenate(part, axis=0))
        return jnp.concatenate(parts, axis=1)

    def layer_two(r, parts=(0, 1)):
        base = r * pitch if isinstance(r, int) else pl.multiple_of(r * pitch, SEGS)
        for pieces in [(((0, half_at),), ((half_at, right_end), (plan.left_at, left_end)))[p] for p in parts]:
            value = jnp.dot(patch_two(base, pieces), w2_ref[...], preferred_element_type=F32)
            value = jax.nn.relu(value + b_ref[1:2, :])
            if isinstance(r, int) and r in (0, 8):
                group_row = iota((1, plan.lanes), 1) // (2 * ch)
                keep = jnp.where(group_row == r // 8, top_row if r == 0 else end_row, 1.0)
                value = value * keep
            start = 0
            for low, high in pieces:
                piece = value[start : start + high - low]
                start += high - low
                for (seg, at, edges) in areas:
                    end = at + (seg // 2 + 1) * SEGS
                    if low == at:
                        first = piece[:SEGS]
                        piece = jnp.concatenate([jnp.where(odd == 0, first * edges[0], first), piece[SEGS:]], axis=0)
                    if high == end:
                        last = piece[high - low - SEGS :]
                        piece = jnp.concatenate(
                            [piece[: high - low - SEGS], jnp.where(odd == 1, last * edges[1], last)], axis=0
                        )
                x2_ref[pl.ds(base + low, high - low)] = piece.astype(BF16)

    for step in range(5):
        layer_one(step)
    for r in range(4):
        if r + 5 < 10:
            layer_one(r + 5)
        layer_two(r)
    layer_one(9)

    per = plan.quads_left * SEGS
    group = iota((per, plan.lanes), 1) // ch

    chunk = 256
    chunks = plan.points // chunk

    def patch(r, at, count):
        base = r * pitch + at
        return jnp.concatenate(
            [
                x2_ref[pl.ds(pl.multiple_of(base + (k // 2) * pitch + (k % 2) * SEGS, SEGS), count)]
                for k in range(4)
            ],
            axis=1,
        )

    def layer_three(r, slot, u):
        rows_in = patch(r, u * chunk, chunk)
        if u == 0:
            rows_in = jnp.concatenate([rows_in, patch(r, plan.left_at, per)], axis=0)
        value = jnp.dot(rows_in, w3_ref[...], preferred_element_type=F32) + b_ref[2:3, :]
        x3_ref[slot, u * chunk : (u + 1) * chunk] = value[:chunk].astype(BF16)
        if u:
            return
        left = value[chunk:]
        swapped = jnp.concatenate(
            [left[:, ch : 2 * ch], left[:, :ch], left[:, 3 * ch :], left[:, 2 * ch : 3 * ch]], axis=1
        )
        for block in range(8):
            dy, dxr, dxl = block // 4, (block // 2) % 2, block % 2
            piece = jnp.where(group == 2 * dy + dxr, left if dxl == dxr else swapped, 0.0)
            lb_ref[slot, block * per : (block + 1) * per] = piece.astype(BF16)

    scale = math.log2(math.e) / math.sqrt(ch)
    pair = 2 * per
    step = 32

    def multiply(slot, u, top):
        value = lax.dot_general(
            x3_ref[slot, u * chunk : (u + 1) * chunk], lb_ref[slot], NT, preferred_element_type=F32
        )
        for at in range(0, chunk, step):
            row_at = slice(u * chunk + at, u * chunk + at + step)
            mask = mask_ref[row_at, :]
            piece = value[at : at + step] + jnp.concatenate([mask, mask], axis=1)
            s_ref[slot, row_at, :] = piece
            best = jnp.max(piece.reshape(step // 8, 8, 4 * pair), axis=0)
            top = best if top is None else jnp.maximum(top, best)
        return top

    def spread_top(top):
        top = jnp.max(top, axis=0, keepdims=True)
        parts = []
        for dy in range(2):
            low, high = top[:, 2 * dy * pair : (2 * dy + 1) * pair], top[:, (2 * dy + 1) * pair : (2 * dy + 2) * pair]
            parts += [jnp.maximum(low, high)] * 2
        return jnp.broadcast_to(jnp.concatenate(parts, axis=1), (8, 4 * pair))

    def weigh(slot, u, top, state):
        state = list(state)
        for at in range(0, chunk, step):
            row_at = slice(u * chunk + at, u * chunk + at + step)
            disp = disp_ref[row_at, :].reshape(step // 8, 8, 2 * pair)
            for dy in range(2):
                lanes = slice(dy * 2 * pair, (dy + 1) * 2 * pair)
                value = s_ref[slot, row_at, lanes].reshape(step // 8, 8, 2 * pair)
                weight = jnp.exp2((value - top[:, lanes][None]) * scale)
                state[2 * dy] = state[2 * dy] + jnp.sum(weight, axis=0)
                state[2 * dy + 1] = state[2 * dy + 1] + jnp.sum(weight * disp, axis=0)
        return state

    def keep_sums(r, state):
        for dy in range(2):
            for target, value in ((tot_ref, state[2 * dy]), (mom_ref, state[2 * dy + 1])):
                value = jnp.sum(value, axis=0, keepdims=True)
                target[2 * r + dy : 2 * r + dy + 1, :] = value[:, :pair] + value[:, pair:]

    none = [jnp.zeros((8, 2 * pair), F32)] * 4
    for u in range(chunks):
        layer_three(0, 0, u)

    top = None
    for r in range(9):
        slot, state, later = r % 2, none, None
        for u in range(chunks):
            if r + 4 < 9:
                layer_two(r + 4, range(u * 2 // chunks, (u + 1) * 2 // chunks))
            if r > 0:
                state = weigh(1 - slot, u, top, state)
            if r < 7:
                layer_three(r + 1, 1 - slot, u)
            if r < 8:
                later = multiply(slot, u, later)
        if r > 0:
            keep_sums(r - 1, state)
        top = spread_top(later) if r < 8 else None

    n, p = iota((pair, cols), 0), iota((pair, cols), 1)
    left = n % per
    place = (left % SEGS) * plan.seg_left + 2 * (left // SEGS) + n // per
    turn = jnp.where(place == p, 1.0, 0.0).astype(F32)
    value = mom_ref[...] / tot_ref[...] * (1.0 / cols)
    out_ref[...] = jnp.dot(value, turn, precision=lax.Precision.HIGHEST, preferred_element_type=F32)


def solution(mesh):
    def per_device(
        left_image, right_image, kernel_one, bias_one, kernel_two, bias_two,
        kernel_three, bias_three, block_list, block_count,
    ):
        rows, cols = left_image.shape
        ch = kernel_one.shape[0]
        plan = Plan(mesh, rows, cols, ch)
        devices = plan.n_row * plan.n_col
        message = pl.pallas_call(
            pack_kernel,
            out_shape=jax.ShapeDtypeStruct((devices, rows + 8, cols), BF16),
        )(left_image, right_image)
        gathered = lax.all_to_all(message, ("row", "col"), 0, 0)
        vmem = pl.BlockSpec(memory_space=pltpu.VMEM)
        smem = pl.BlockSpec(memory_space=pltpu.SMEM)
        lanes = plan.lanes
        n_left = 4 * SEGS * plan.quads_left
        w1, w2, w3, biases, mask, disp, spread, own = pl.pallas_call(
            functools.partial(prep_kernel, plan),
            out_shape=(
                jax.ShapeDtypeStruct((5, 256, lanes), BF16),
                jax.ShapeDtypeStruct((4 * lanes, lanes), BF16),
                jax.ShapeDtypeStruct((4 * lanes, lanes), BF16),
                jax.ShapeDtypeStruct((3, lanes), F32),
                jax.ShapeDtypeStruct((plan.points, n_left), F32),
                jax.ShapeDtypeStruct((plan.points, n_left), F32),
                jax.ShapeDtypeStruct((256, 512), BF16),
                jax.ShapeDtypeStruct((rows, cols), F32),
            ),
            in_specs=[vmem] * 7 + [smem, smem],
            out_specs=(vmem,) * 8,
            compiler_params=pltpu.CompilerParams(vmem_limit_bytes=(12 if plan.ring else 24) * 2**20),
        )(
            left_image, kernel_one.T, bias_one[None], kernel_two, bias_two[None], kernel_three, bias_three[None],
            block_list.reshape(-1), block_count.reshape(-1),
        )
        return pl.pallas_call(
            functools.partial(main_kernel, plan),
            out_shape=jax.ShapeDtypeStruct((rows, cols), F32),
            in_specs=[vmem] * 9,
            out_specs=vmem,
            scratch_shapes=[
                pltpu.VMEM((3 * rows, (plan.tiles + 3) * cols), F32),
                pltpu.VMEM((256, (plan.tiles + 3) * cols), BF16),
                pltpu.VMEM((plan.total, 256), BF16),
                pltpu.VMEM((2, plan.total, 256), BF16),
                pltpu.VMEM((10 * plan.total, lanes), BF16),
                pltpu.VMEM((10 * plan.total, lanes), BF16),
                pltpu.VMEM((2, plan.points, lanes), BF16),
                pltpu.VMEM((2, 2 * n_left, lanes), BF16),
                pltpu.VMEM((2, plan.points, 2 * n_left), F32),
                pltpu.VMEM((rows, cols), F32),
                pltpu.VMEM((rows, cols), F32),
            ],
            compiler_params=pltpu.CompilerParams(vmem_limit_bytes=(18 if plan.ring else 44) * 2**20),
        )(gathered, own, spread, w1, biases, w2, w3, mask, disp)

    return jax.shard_map(
        per_device,
        mesh=mesh,
        in_specs=(
            P("row", "col"), P("row", "col"), P(), P(), P(), P(), P(), P(),
            P("row", "col", None), P("row", "col"),
        ),
        out_specs=P("row", "col"),
        check_vma=False,
    )
```

```python
import functools
import math

import jax
import jax.numpy as jnp
from jax import lax
from jax.experimental import pallas as pl
from jax.experimental.pallas import tpu as pltpu
from jax.sharding import PartitionSpec as P

DBLOCK = 64
SPAN = 4
SEGS = 16
NT = (((1,), (1,)), ((), ()))
F32 = jnp.float32
BF16 = jnp.bfloat16


def iota(shape, dim):
    return lax.broadcasted_iota(jnp.int32, shape, dim)


class Plan:
    def __init__(self, mesh, rows, cols, chans):
        self.n_row, self.n_col = mesh.shape["row"], mesh.shape["col"]
        self.rows, self.cols, self.chans = rows, cols, chans
        self.ring = self.n_col == 2 * SPAN
        self.tiles = self.n_col if self.ring else 16
        self.width = self.n_col * cols
        self.seg = self.tiles * cols // SEGS
        self.quads = self.seg // 2
        self.seg_left = cols // SEGS
        self.quads_left = self.seg_left // 2
        self.left_at = (self.quads + 2) * SEGS
        self.total = self.left_at + (self.quads_left + 2) * SEGS
        self.points = self.quads * SEGS
        self.lanes = 4 * chans


def pack_kernel(left_ref, right_ref, out_ref):
    rows, cols = left_ref.shape
    left = left_ref[...]
    edges = []
    for first in (0, cols - 3):
        lane, n = iota((cols, cols), 0), iota((cols, cols), 1)
        pick = jnp.where(lane == first + n // rows, 1.0, 0.0).astype(BF16)
        value = jnp.dot(left, pick, preferred_element_type=F32)
        y, n = iota((rows, cols), 0), iota((rows, cols), 1)
        value = jnp.where((y == n % rows) & (n < 3 * rows), value, 0.0)
        edges.append(jnp.sum(value, axis=0, keepdims=True))
    left = left.astype(F32)
    message = jnp.concatenate(
        [right_ref[...].astype(F32), left[:3], left[rows - 3 :]] + edges, axis=0
    ).astype(BF16)
    for k in range(out_ref.shape[0]):
        out_ref[k] = message


def prep_kernel(
    plan, left_ref, k1_ref, b1_ref, k2_ref, b2_ref, k3_ref, b3_ref, list_ref, count_ref,
    w1_ref, w2_ref, w3_ref, b_ref, mask_ref, disp_ref, spread_ref, own_ref,
):
    ch = plan.chans
    own_ref[...] = left_ref[...].astype(F32)
    kernel = k1_ref[...]
    high = kernel.astype(BF16)
    rest = kernel - high.astype(F32)
    middle = rest.astype(BF16)
    low = (rest - middle.astype(F32)).astype(BF16)
    taps = kernel.shape[0]
    w1_ref[...] = jnp.zeros(w1_ref.shape, BF16)
    for part, values in enumerate((high, middle, low)):
        for out in range(4):
            oy, ox = divmod(out, 2)
            row, tap = iota((5 * 64, taps), 0), iota((5 * 64, taps), 1)
            step, px, y = row // 64, (row // 16) % 4, row % 16
            pick = (px == tap % 3 + ox) & (y == 2 * step + oy + tap // 3)
            pick = jnp.where(pick, 1.0, 0.0).astype(BF16)
            block = jnp.dot(pick, values, preferred_element_type=F32).astype(BF16)
            for step in range(5):
                w1_ref[step, part * 64 : part * 64 + 64, out * ch : out * ch + ch] = block[
                    step * 64 : step * 64 + 64
                ]
    for layer, bias in enumerate((b1_ref, b2_ref, b3_ref)):
        b_ref[layer : layer + 1, :] = jnp.concatenate([bias[...]] * 4, axis=1)
    for source, target in ((k2_ref, w2_ref), (k3_ref, w3_ref)):
        turned = [source[tap].astype(F32).T for tap in range(9)]
        nothing = jnp.zeros((ch, ch), F32)
        for py in range(4):
            for px in range(4):
                pieces = []
                for out in range(4):
                    ty, tx = py - out // 2, px - out % 2
                    inside = 0 <= ty < 3 and 0 <= tx < 3
                    pieces.append(turned[3 * ty + tx] if inside else nothing)
                quad, sub = (py // 2) * 2 + px // 2, (py % 2) * 2 + px % 2
                at = (4 * quad + sub) * ch
                target[at : at + ch, :] = jnp.concatenate(pieces, axis=1).astype(BF16)
    col = lax.axis_index("col")
    bits = jnp.int32(0)
    for k in range(list_ref.shape[0]):
        bits = bits | jnp.where(k < count_ref[0], jnp.left_shift(jnp.int32(1), list_ref[k]), 0)
    reach = SPAN * plan.cols
    shape = (plan.points, 4 * SEGS * plan.quads_left)
    m, n = iota(shape, 0), iota(shape, 1)
    per = SEGS * plan.quads_left
    q = (m % SEGS) * plan.seg + 2 * (m // SEGS) + n // (2 * per)
    left = n % per
    p = (left % SEGS) * plan.seg_left + 2 * (left // SEGS) + (n // per) % 2
    if plan.ring:
        d = col * plan.cols + p - q
        d = jnp.where(d < -reach, d + plan.width, d)
        d = jnp.where(d >= reach, d - plan.width, d)
        listed = jnp.right_shift(bits, (d + reach) // DBLOCK) & 1
    else:
        d = 5 * plan.cols + p - q
        inside = (d >= -reach) & (d < reach)
        block = jnp.where(inside, (d + reach) // DBLOCK, 31)
        listed = jnp.where(inside, jnp.right_shift(bits, block) & 1, 0)
    mask_ref[...] = jnp.where(listed > 0, 0.0, -1e30).astype(F32)
    disp_ref[...] = d.astype(F32)

    row = lax.axis_index("row")
    k, n = iota((256, 1), 0), iota((1, 512), 1)
    y = 10 * (n // 256) + n % 16
    wanted = jnp.where((y < plan.rows + 6) & (n % 256 < 192), (n // 16) % 4 * 64 + plan.rows - 3 + y, -1)
    v = k % 64
    hidden = ((row == 0) & (v < plan.rows)) | ((row == plan.n_row - 1) & (v >= 2 * plan.rows))
    spread_ref[...] = jnp.where(wanted == jnp.where(hidden, -2, k), 1.0, 0.0).astype(BF16)


def main_kernel(
    plan, g_ref, left_ref, spread_ref, w1_ref, b_ref, w2_ref, w3_ref, mask_ref, disp_ref, out_ref,
    v_ref, v4_ref, fx_ref, f_ref, x1_ref, x2_ref, x3_ref, lb_ref, s_ref, tot_ref, mom_ref,
):
    rows, cols, ch = plan.rows, plan.cols, plan.chans
    row, col = lax.axis_index("row"), lax.axis_index("col")
    first_row, last_row = row == 0, row == plan.n_row - 1

    def message(dr, tile):
        return g_ref[jnp.clip(row + dr, 0, plan.n_row - 1) * plan.n_col + tile].astype(F32)

    wide = plan.tiles * cols
    for t in range(plan.tiles):
        tile = t if plan.ring else lax.rem(col + (t - 5 + plan.n_col), plan.n_col)
        for dr in range(3):
            v_ref[dr * rows : (dr + 1) * rows, t * cols : (t + 1) * cols] = message(dr - 1, tile)[:rows]
    seg_id = iota((SEGS, 1), 0)
    if plan.ring:
        begin = seg_id * plan.seg
    else:
        begin = lax.rem((col + plan.n_col - 5) * cols + seg_id * plan.seg, plan.width)
    edges_right = (
        jnp.where(begin == 0, 0.0, 1.0).astype(F32),
        jnp.where(begin + plan.seg == plan.width, 0.0, 1.0).astype(F32),
    )
    edges_left = (
        jnp.where((col == 0) & (seg_id == 0), 0.0, 1.0).astype(F32),
        jnp.where((col == plan.n_col - 1) & (seg_id == SEGS - 1), 0.0, 1.0).astype(F32),
    )
    areas = (
        (plan.seg, 0, edges_right),
        (plan.seg_left, plan.left_at, edges_left),
    )
    px_lane = iota((SEGS, 256), 1) // 64

    def patches(start, before, size, area):
        seg, at, edges = area
        for px in range(4):
            moved = v_ref[:, start : start + size]
            moved = moved if px == 1 else pltpu.roll(moved, (1 - px) % size, 1)
            v4_ref[px * 64 : px * 64 + 3 * rows, start : start + size] = moved.astype(BF16)
            v4_ref[px * 64 + 3 * rows : px * 64 + 64, start : start + size] = jnp.zeros((64 - 3 * rows, size), BF16)
        count = (seg // 2 + 2) * SEGS
        n, k = iota((count, 1), 0), iota((1, size), 1)
        pick = jnp.where(before + (n % SEGS) * seg + 2 * (n // SEGS) - 2 == k, 1.0, 0.0).astype(BF16)
        value = lax.dot_general(pick, v4_ref[:, start : start + size], NT, preferred_element_type=F32)
        fx_ref[at : at + count, :] = value.astype(BF16)
        low = value[SEGS : 2 * SEGS]
        fx_ref[at + SEGS : at + 2 * SEGS, :] = jnp.where(px_lane == 0, low * edges[0], low).astype(BF16)
        high = value[count - 2 * SEGS : count - SEGS]
        fx_ref[at + count - 2 * SEGS : at + count - SEGS, :] = jnp.where(
            px_lane == 3, high * edges[1], high
        ).astype(BF16)

    patches(0, 0, wide, areas[0])
    blank = jnp.zeros((rows - 3, cols), F32)
    for t in range(3):
        tile = lax.rem(col + (t - 1 + plan.n_col), plan.n_col)
        at = slice(wide + t * cols, wide + (t + 1) * cols)
        v_ref[0:rows, at] = jnp.concatenate([blank, message(-1, tile)[rows + 3 : rows + 6]], axis=0)
        v_ref[2 * rows : 3 * rows, at] = jnp.concatenate([message(1, tile)[rows : rows + 3], blank], axis=0)
        if t == 1:
            v_ref[rows : 2 * rows, at] = left_ref[...]
        else:
            edge = jnp.broadcast_to(message(0, tile)[rows + (7 if t == 0 else 6) :][:1], (rows, cols))
            y, n = iota((rows, cols), 0), iota((rows, cols), 1)
            edge = jnp.where((y == n % rows) & (n < 3 * rows), edge, 0.0).astype(BF16)
            n, lane = iota((cols, cols), 0), iota((cols, cols), 1)
            pick = jnp.where((lane == (cols - 3 if t == 0 else 0) + n // rows) & (n < 3 * rows), 1.0, 0.0)
            v_ref[rows : 2 * rows, at] = jnp.dot(edge, pick.astype(BF16), preferred_element_type=F32)
    patches(wide, cols, 3 * cols, areas[1])
    def spread_half(half):
        value = jnp.dot(
            fx_ref[...], spread_ref[:, half * 256 : half * 256 + 256], preferred_element_type=F32
        )
        f_ref[half] = value.astype(BF16)

    spread_half(0)

    def clear_first(value):
        pieces = []
        for seg, at, edges in areas:
            end = at + (seg // 2 + 2) * SEGS
            pieces.append(value[at : at + SEGS] * edges[0])
            pieces.append(value[at + SEGS : end - SEGS])
            pieces.append(value[end - SEGS : end] * edges[1])
        return jnp.concatenate(pieces, axis=0)

    pitch = plan.total

    top_row = jnp.where(first_row, 0.0, 1.0).astype(F32)
    end_row = jnp.where(last_row, 0.0, 1.0).astype(F32)
    def layer_one(step):
        value = jnp.dot(f_ref[step // 5], w1_ref[step % 5], preferred_element_type=F32)
        value = clear_first(jax.nn.relu(value + b_ref[0:1, :]))
        if step == 0:
            value = value * top_row
        if step == 9:
            value = value * end_row
        x1_ref[step * pitch : (step + 1) * pitch] = value.astype(BF16)


    odd = (iota((SEGS, plan.lanes), 1) // ch) % 2

    half_at = (plan.quads + 1) // 2 * SEGS + 3 * SEGS
    right_end = (plan.quads + 1) * SEGS
    left_end = plan.left_at + (plan.quads_left + 1) * SEGS

    def patch_two(base, pieces):
        parts = []
        for k in range(4):
            at = base + (k // 2) * pitch + (k % 2) * SEGS
            part = [x1_ref[pl.ds(at + low, high - low)] for low, high in pieces]
            parts.append(part[0] if len(part) == 1 else jnp.concatenate(part, axis=0))
        return jnp.concatenate(parts, axis=1)

    def layer_two(r, parts=(0, 1)):
        base = r * pitch if isinstance(r, int) else pl.multiple_of(r * pitch, SEGS)
        for pieces in [(((0, half_at),), ((half_at, right_end), (plan.left_at, left_end)))[p] for p in parts]:
            value = jnp.dot(patch_two(base, pieces), w2_ref[...], preferred_element_type=F32)
            value = jax.nn.relu(value + b_ref[1:2, :])
            if isinstance(r, int) and r in (0, 8):
                group_row = iota((1, plan.lanes), 1) // (2 * ch)
                keep = jnp.where(group_row == r // 8, top_row if r == 0 else end_row, 1.0)
                value = value * keep
            start = 0
            for low, high in pieces:
                piece = value[start : start + high - low]
                start += high - low
                for (seg, at, edges) in areas:
                    end = at + (seg // 2 + 1) * SEGS
                    if low == at:
                        first = piece[:SEGS]
                        piece = jnp.concatenate([jnp.where(odd == 0, first * edges[0], first), piece[SEGS:]], axis=0)
                    if high == end:
                        last = piece[high - low - SEGS :]
                        piece = jnp.concatenate(
                            [piece[: high - low - SEGS], jnp.where(odd == 1, last * edges[1], last)], axis=0
                        )
                x2_ref[pl.ds(base + low, high - low)] = piece.astype(BF16)

    for step in range(5):
        layer_one(step)
        if step == 1:
            spread_half(1)
    for r in range(4):
        if r + 5 < 10:
            layer_one(r + 5)
        layer_two(r)
    layer_one(9)

    per = plan.quads_left * SEGS
    group = iota((per, plan.lanes), 1) // ch

    chunk = 256
    chunks = plan.points // chunk

    def patch(r, at, count):
        base = r * pitch + at
        return jnp.concatenate(
            [
                x2_ref[pl.ds(pl.multiple_of(base + (k // 2) * pitch + (k % 2) * SEGS, SEGS), count)]
                for k in range(4)
            ],
            axis=1,
        )

    def layer_three(r, slot, u):
        rows_in = patch(r, u * chunk, chunk)
        if u == 0:
            rows_in = jnp.concatenate([rows_in, patch(r, plan.left_at, per)], axis=0)
        value = jnp.dot(rows_in, w3_ref[...], preferred_element_type=F32) + b_ref[2:3, :]
        x3_ref[slot, u * chunk : (u + 1) * chunk] = value[:chunk].astype(BF16)
        if u:
            return
        left = value[chunk:]
        swapped = jnp.concatenate(
            [left[:, ch : 2 * ch], left[:, :ch], left[:, 3 * ch :], left[:, 2 * ch : 3 * ch]], axis=1
        )
        for block in range(8):
            dy, dxr, dxl = block // 4, (block // 2) % 2, block % 2
            piece = jnp.where(group == 2 * dy + dxr, left if dxl == dxr else swapped, 0.0)
            lb_ref[slot, block * per : (block + 1) * per] = piece.astype(BF16)

    scale = math.log2(math.e) / math.sqrt(ch)
    pair = 2 * per
    step = 32

    def multiply(slot, u, top):
        value = lax.dot_general(
            x3_ref[slot, u * chunk : (u + 1) * chunk], lb_ref[slot], NT, preferred_element_type=F32
        )
        for at in range(0, chunk, step):
            row_at = slice(u * chunk + at, u * chunk + at + step)
            mask = mask_ref[row_at, :]
            piece = value[at : at + step] + jnp.concatenate([mask, mask], axis=1)
            s_ref[slot, row_at, :] = piece
            best = jnp.max(piece.reshape(step // 8, 8, 4 * pair), axis=0)
            top = best if top is None else jnp.maximum(top, best)
        return top

    def spread_top(top):
        top = jnp.max(top, axis=0, keepdims=True)
        parts = []
        for dy in range(2):
            low, high = top[:, 2 * dy * pair : (2 * dy + 1) * pair], top[:, (2 * dy + 1) * pair : (2 * dy + 2) * pair]
            parts += [jnp.maximum(low, high)] * 2
        return jnp.broadcast_to(jnp.concatenate(parts, axis=1), (8, 4 * pair))

    def weigh(slot, u, top, state):
        state = list(state)
        for at in range(0, chunk, step):
            row_at = slice(u * chunk + at, u * chunk + at + step)
            disp = disp_ref[row_at, :].reshape(step // 8, 8, 2 * pair)
            for dy in range(2):
                lanes = slice(dy * 2 * pair, (dy + 1) * 2 * pair)
                value = s_ref[slot, row_at, lanes].reshape(step // 8, 8, 2 * pair)
                weight = jnp.exp2((value - top[:, lanes][None]) * scale)
                state[2 * dy] = state[2 * dy] + jnp.sum(weight, axis=0)
                state[2 * dy + 1] = state[2 * dy + 1] + jnp.sum(weight * disp, axis=0)
        return state

    def keep_sums(r, state):
        for dy in range(2):
            for target, value in ((tot_ref, state[2 * dy]), (mom_ref, state[2 * dy + 1])):
                value = jnp.sum(value, axis=0, keepdims=True)
                target[2 * r + dy : 2 * r + dy + 1, :] = value[:, :pair] + value[:, pair:]

    none = [jnp.zeros((8, 2 * pair), F32)] * 4
    for u in range(chunks):
        layer_three(0, 0, u)

    n, p = iota((pair, cols), 0), iota((pair, cols), 1)
    left = n % per
    place = (left % SEGS) * plan.seg_left + 2 * (left // SEGS) + n // per
    turn = jnp.where(place == p, 1.0, 0.0).astype(BF16)
    top = None
    for r in range(9):
        slot, state, later = r % 2, none, None
        for u in range(chunks):
            if r + 4 < 9:
                layer_two(r + 4, range(u * 2 // chunks, (u + 1) * 2 // chunks))
            if r > 0:
                state = weigh(1 - slot, u, top, state)
            if r < 7:
                layer_three(r + 1, 1 - slot, u)
            if r < 8:
                later = multiply(slot, u, later)
        if r > 0:
            keep_sums(r - 1, state)
        top = spread_top(later) if r < 8 else None

    value = mom_ref[...] / tot_ref[...] * (1.0 / cols)
    high = value.astype(BF16)
    rest = value - high.astype(F32)
    middle = rest.astype(BF16)
    low = (rest - middle.astype(F32)).astype(BF16)
    parts = jnp.concatenate([high, middle, low], axis=1)
    out_ref[...] = jnp.dot(parts, jnp.concatenate([turn] * 3, axis=0), preferred_element_type=F32)


def solution(mesh):
    def per_device(
        left_image, right_image, kernel_one, bias_one, kernel_two, bias_two,
        kernel_three, bias_three, block_list, block_count,
    ):
        rows, cols = left_image.shape
        ch = kernel_one.shape[0]
        plan = Plan(mesh, rows, cols, ch)
        devices = plan.n_row * plan.n_col
        message = pl.pallas_call(
            pack_kernel,
            out_shape=jax.ShapeDtypeStruct((devices, rows + 8, cols), BF16),
        )(left_image, right_image)
        gathered = lax.all_to_all(message, ("row", "col"), 0, 0)
        vmem = pl.BlockSpec(memory_space=pltpu.VMEM)
        smem = pl.BlockSpec(memory_space=pltpu.SMEM)
        lanes = plan.lanes
        n_left = 4 * SEGS * plan.quads_left
        w1, w2, w3, biases, mask, disp, spread, own = pl.pallas_call(
            functools.partial(prep_kernel, plan),
            out_shape=(
                jax.ShapeDtypeStruct((5, 256, lanes), BF16),
                jax.ShapeDtypeStruct((4 * lanes, lanes), BF16),
                jax.ShapeDtypeStruct((4 * lanes, lanes), BF16),
                jax.ShapeDtypeStruct((3, lanes), F32),
                jax.ShapeDtypeStruct((plan.points, n_left), F32),
                jax.ShapeDtypeStruct((plan.points, n_left), F32),
                jax.ShapeDtypeStruct((256, 512), BF16),
                jax.ShapeDtypeStruct((rows, cols), F32),
            ),
            in_specs=[vmem] * 7 + [smem, smem],
            out_specs=(vmem,) * 8,
            compiler_params=pltpu.CompilerParams(vmem_limit_bytes=(12 if plan.ring else 24) * 2**20),
        )(
            left_image, kernel_one.T, bias_one[None], kernel_two, bias_two[None], kernel_three, bias_three[None],
            block_list.reshape(-1), block_count.reshape(-1),
        )
        return pl.pallas_call(
            functools.partial(main_kernel, plan),
            out_shape=jax.ShapeDtypeStruct((rows, cols), F32),
            in_specs=[vmem] * 9,
            out_specs=vmem,
            scratch_shapes=[
                pltpu.VMEM((3 * rows, (plan.tiles + 3) * cols), F32),
                pltpu.VMEM((256, (plan.tiles + 3) * cols), BF16),
                pltpu.VMEM((plan.total, 256), BF16),
                pltpu.VMEM((2, plan.total, 256), BF16),
                pltpu.VMEM((10 * plan.total, lanes), BF16),
                pltpu.VMEM((10 * plan.total, lanes), BF16),
                pltpu.VMEM((2, plan.points, lanes), BF16),
                pltpu.VMEM((2, 2 * n_left, lanes), BF16),
                pltpu.VMEM((2, plan.points, 2 * n_left), F32),
                pltpu.VMEM((rows, cols), F32),
                pltpu.VMEM((rows, cols), F32),
            ],
            compiler_params=pltpu.CompilerParams(vmem_limit_bytes=(18 if plan.ring else 44) * 2**20),
        )(gathered, own, spread, w1, biases, w2, w3, mask, disp)

    return jax.shard_map(
        per_device,
        mesh=mesh,
        in_specs=(
            P("row", "col"), P("row", "col"), P(), P(), P(), P(), P(), P(),
            P("row", "col", None), P("row", "col"),
        ),
        out_specs=P("row", "col"),
        check_vma=False,
    )
```
